256 devices in a mesh: line: 16 (over z_hi, x, core), shot: 16 (over z_lo, y).
Axes of the slice: x: 4, y: 4, z: 8 (z_hi: 2, z_lo: 4; z = z_hi * 4 + z_lo), core: 2. Of those that a mesh axis runs over, the one named last changes fastest.
Arguments:
- velocity: float32 [256, 256, 128], P('line', 'shot'), may hold values from 1.5 to 4.5
- density: float32 [256, 256, 128], P('line', 'shot'), may hold values from 1 to 3
- start_pressure: float32 [512, 512, 128], P('line', 'shot'), may hold values from -6 to 6
- observed: float32 [512, 512, 128], P('line', 'shot'), may hold values from -6 to 6
- corners: int32 [16, 16, 2], P('line', 'shot'), may hold values from 0 to 224, as said below
Outputs:
- grad_velocity: float32 [256, 256, 128], P('line', 'shot')
- grad_density: float32 [256, 256, 128], P('line', 'shot')
The draws below stay inside these ranges and needn't reach their ends.
Inputs may be any that keep to these rules, and one draw needn't show every extreme that they name: corners[a, b, 0] = min(max(a * 16 - 16 + r, 0), 224) and corners[a, b, 1] = min(max(b * 16 - 16 + t, 0), 224) for whole numbers r and t of 0 to 16.
All inputs are finite; a program needn't handle non-finite values.
Results may differ from the reference program's by a relative error of at most 0.0003.
Values sent between devices are 32-bit elements; how exact they have to be, the bound alone decides.
No kernel may reach another device: no remote copies, remote signals or barrier semaphores. Data moves between devices by JAX's collectives and lax.ppermute only.
A program may use at most 64 MiB of HBM per device.

```python
import math
import jax
import jax.numpy as jnp
from jax import lax

BLOCK = 16
NZ = 128
APER = 32
GX = 256
GY = 256
N_LINE = 16
N_SHOT = 16


def draw_corners(key, part):
    offsets = jax.random.randint(key, (N_LINE, N_SHOT, 2), 0, BLOCK + 1)
    line_ids = jnp.arange(N_LINE, dtype=jnp.int32)[:, None]
    shot_ids = jnp.arange(N_SHOT, dtype=jnp.int32)[None, :]
    first = jnp.clip(line_ids * BLOCK - BLOCK + offsets[:, :, 0], 0, GX - 2 * BLOCK)
    second = jnp.clip(shot_ids * BLOCK - BLOCK + offsets[:, :, 1], 0, GY - 2 * BLOCK)
    return jnp.stack([first, second], axis=-1).astype(jnp.int32)


def levels(stream_key, extent, shards, least, largest):
    factor_of, own = 1.0, jax.random.fold_in(stream_key, 6)
    for axis_at, parts in shards:
        draws = jnp.exp(jax.random.uniform(jax.random.fold_in(own, axis_at), (parts,), jnp.float32, least / len(shards), largest / len(shards)))
        factor_of = factor_of * jnp.repeat(draws, extent[axis_at] // parts).reshape([-1 if axis == axis_at else 1 for axis in range(len(extent))])
    return factor_of


def noise(key, shape, scale, bound, cuts=(), held_as=jnp.bfloat16):
    array = scale * jax.random.normal(key, shape, jnp.float32)
    if cuts:
        array = array * levels(key, shape, cuts, -0.22, 0.18)
    return jnp.clip(array, -bound, bound).astype(held_as)


def setup_inputs(seed: int = 0) -> dict:
    keys = jax.random.split(jax.random.key(seed), 6)
    return {
        "velocity": jnp.clip(1.5 + 3.0 * jax.random.uniform(keys[0], (GX, GY, NZ), jnp.float32) ** levels(keys[0], (GX, GY, NZ), ((0, 16), (1, 16)), -0.2, 0.2), 1.5, 4.5),
        "density": jnp.clip(jnp.exp(math.log(3.0) - 1.0986123 * jax.random.uniform(keys[1], (GX, GY, NZ), jnp.float32) ** levels(keys[1], (GX, GY, NZ), ((0, 16), (1, 16)), -0.2, 0.2)), 1.0, 3.0),
        "start_pressure": noise(keys[2], (N_LINE * APER, N_SHOT * APER, NZ), 1.0, 6.0, ((0, 16), (1, 16)), jnp.float32),
        "observed": noise(keys[3], (N_LINE * APER, N_SHOT * APER, NZ), 1.0, 6.0, ((0, 16), (1, 16)), jnp.float32),
        "corners": draw_corners(jax.random.fold_in(keys[5], 71), 0),
    }


coeffs = (1225.0 / 1024.0, -245.0 / 3072.0, 49.0 / 5120.0, -5.0 / 7168.0)
time_ratio = 0.1
wavelet = (20.0, -12.0)

def deriv_plus(field, axis):
    widths = [(0, 0)] * 3
    widths[axis] = (4, 4)
    padded = jnp.pad(field, widths)
    count = field.shape[axis]
    total = jnp.zeros_like(field)
    for m in range(1, 5):
        upper = lax.slice_in_dim(padded, 4 + m, 4 + m + count, axis=axis)
        lower = lax.slice_in_dim(padded, 5 - m, 5 - m + count, axis=axis)
        total = total + coeffs[m - 1] * (upper - lower)
    return total

def deriv_minus(field, axis):
    widths = [(0, 0)] * 3
    widths[axis] = (4, 4)
    padded = jnp.pad(field, widths)
    count = field.shape[axis]
    total = jnp.zeros_like(field)
    for m in range(1, 5):
        upper = lax.slice_in_dim(padded, 3 + m, 3 + m + count, axis=axis)
        lower = lax.slice_in_dim(padded, 4 - m, 4 - m + count, axis=axis)
        total = total + coeffs[m - 1] * (upper - lower)
    return total

def shot_misfit(model, pressure, observed):
    speed = model[0]
    dense = model[1]
    vel_x = jnp.zeros_like(pressure)
    vel_y = jnp.zeros_like(pressure)
    vel_z = jnp.zeros_like(pressure)
    centre = (pressure.shape[0] // 2, pressure.shape[1] // 2, pressure.shape[2] // 2)
    for level in range(2):
        vel_x = vel_x - time_ratio * deriv_plus(pressure, 0) / dense
        vel_y = vel_y - time_ratio * deriv_plus(pressure, 1) / dense
        vel_z = vel_z - time_ratio * deriv_plus(pressure, 2) / dense
        spread = deriv_minus(vel_x, 0) + deriv_minus(vel_y, 1) + deriv_minus(vel_z, 2)
        pressure = pressure - time_ratio * dense * speed * speed * spread
        pressure = pressure.at[centre].add(wavelet[level])
    misfit_term = pressure - observed
    return 0.5 * jnp.sum(misfit_term * misfit_term)

def reference(velocity, density, start_pressure, observed, corners):
    lines = corners.shape[0]
    shots = corners.shape[1]
    depth = velocity.shape[2]
    width = start_pressure.shape[0] // lines
    model = jnp.stack([velocity, density])
    zero_int = jnp.zeros((), jnp.int32)

    def visit(grads, index):
        line_index = (index // shots).astype(jnp.int32)
        shot_index = (index % shots).astype(jnp.int32)
        corner = corners[line_index, shot_index].astype(jnp.int32)
        place = (zero_int, corner[0], corner[1], zero_int)
        aperture = lax.dynamic_slice(model, place, (2, width, width, depth))
        spot = (line_index * width, shot_index * width, zero_int)
        pressure = lax.dynamic_slice(start_pressure, spot, (width, width, depth))
        seen = lax.dynamic_slice(observed, spot, (width, width, depth))
        local = jax.grad(shot_misfit)(aperture, pressure, seen)
        current = lax.dynamic_slice(grads, place, (2, width, width, depth))
        grads = lax.dynamic_update_slice(grads, current + local, place)
        return (grads, None)
    grads, unused = lax.scan(visit, jnp.zeros_like(model), jnp.arange(lines * shots, dtype=jnp.int32))
    return (grads[0], grads[1])
```

```python
import jax
import jax.numpy as jnp
from jax import lax
from jax.experimental import pallas as pl
from jax.experimental.pallas import tpu as pltpu
from jax.sharding import PartitionSpec as P

coeffs = (1225.0 / 1024.0, -245.0 / 3072.0, 49.0 / 5120.0, -5.0 / 7168.0)
DEPTH_UNIT = coeffs[0] / 105.0
wavelet = (20.0, -12.0)

BLOCK = 16
APER = 32
NZ = 128
ROWS = 4
F32 = jnp.float32


def swap_pairs(odd):
    pairs = []
    for i in range(1 if odd else 0, 15, 2):
        pairs += [(i, i + 1), (i + 1, i)]
    return pairs


def swap(block, axis, odd):
    return lax.ppermute(block, axis, swap_pairs(odd))


def vmem(count):
    return [pl.BlockSpec(memory_space=pltpu.VMEM)] * count


def offset_in_frame(corner_ref, dim, axis):
    return corner_ref[0, 0, dim] - (lax.axis_index(axis) - 1) * BLOCK


def pack_kernel(corner_ref, vel_ref, rho_ref, out_ref):
    out_ref[0:BLOCK] = vel_ref[...]
    out_ref[BLOCK : 2 * BLOCK] = rho_ref[...]
    shift = offset_in_frame(corner_ref, 0, "line").astype(F32)
    out_ref[2 * BLOCK] = jnp.full((BLOCK, NZ), shift, F32)


def pack(corners, velocity, density):
    return pl.pallas_call(
        pack_kernel,
        out_shape=jax.ShapeDtypeStruct((2 * BLOCK + 1, BLOCK, NZ), F32),
        in_specs=[pl.BlockSpec(memory_space=pltpu.SMEM)] + vmem(2),
        out_specs=pl.BlockSpec(memory_space=pltpu.VMEM),
        name="pack",
    )(corners, velocity, density)


def relay_kernel(c_ref, x_ref, ye_ref, yo_ref, oute_ref, outo_ref):
    even = lax.rem(lax.axis_index("line"), 2) == 0
    sign = jnp.where(even, 1.0, -1.0).astype(F32)
    for y_ref, out_ref in ((ye_ref, oute_ref), (yo_ref, outo_ref)):
        shift = y_ref[2 * BLOCK]
        for j in range(BLOCK):
            from_core = (shift - (j + 0.5)) * sign > 0.0
            for f in range(2):
                out_ref[f * BLOCK + j] = jnp.where(from_core, c_ref[f * BLOCK + j], x_ref[f * BLOCK + j])


def relay(c, x, ye, yo):
    shape = jax.ShapeDtypeStruct((2 * BLOCK, BLOCK, NZ), F32)
    return pl.pallas_call(
        relay_kernel,
        out_shape=(shape, shape),
        in_specs=vmem(4),
        out_specs=tuple(vmem(2)),
        name="relay",
    )(c, x, ye, yo)


def stencil(window, rows):
    total = None
    for m in range(1, 5):
        part = coeffs[m - 1] * (window(3 + m) - window(4 - m))
        total = part if total is None else total + part
    return total


def depth_matrix(first):
    source = lax.broadcasted_iota(jnp.int32, (NZ, NZ), 0)
    target = lax.broadcasted_iota(jnp.int32, (NZ, NZ), 1)
    away = source - target + first
    total = jnp.zeros((NZ, NZ), F32)
    for m in range(1, 5):
        value = coeffs[m - 1] / DEPTH_UNIT
        total = jnp.where(away == m, value, total)
        total = jnp.where(away == 1 - m, -value, total)
    half = total.astype(jnp.bfloat16)
    return jnp.concatenate([half, half], axis=0)


def along_depth(values, matrix):
    flat = values.reshape(-1, NZ)
    upper = flat.astype(jnp.bfloat16)
    lower = (flat - upper.astype(F32)).astype(jnp.bfloat16)
    both = jnp.concatenate([upper, lower], axis=1)
    out = jnp.dot(both, matrix, preferred_element_type=F32)
    return (out * DEPTH_UNIT).reshape(values.shape)


def wave_kernel(
    corner_ref, p0_ref, obs_ref, own_ref, c_ref, x_ref, ye_ref, yo_ref, ye2_ref, yo2_ref,
    eh_ref, oh_ref, ew_ref, ow_ref, mh_ref, mw_ref,
    model, terms, field, bx, by, bz, g1, gs, a1, a2, lam, kap, buoy, quad, dens, dplus_mat, dminus_mat,
):
    ox = offset_in_frame(corner_ref, 0, "line")
    oy = offset_in_frame(corner_ref, 1, "shot")
    even_a = lax.rem(lax.axis_index("line"), 2) == 0
    even_b = lax.rem(lax.axis_index("shot"), 2) == 0
    col_e = pl.multiple_of(jnp.where(even_b, 2 * BLOCK, 0), BLOCK)
    col_o = pl.multiple_of(jnp.where(even_b, 0, 2 * BLOCK), BLOCK)

    dplus_mat[...] = depth_matrix(0)
    dminus_mat[...] = depth_matrix(1)

    for f in range(2):
        rows = slice(f * BLOCK, (f + 1) * BLOCK)
        model[f, BLOCK:, BLOCK : 2 * BLOCK] = own_ref[rows]
        model[f, BLOCK:, pl.ds(col_e, BLOCK)] = ye_ref[rows]
        model[f, BLOCK:, pl.ds(col_o, BLOCK)] = yo_ref[rows]
        model[f, :BLOCK, pl.ds(col_e, BLOCK)] = ye2_ref[rows]
        model[f, :BLOCK, pl.ds(col_o, BLOCK)] = yo2_ref[rows]
        for j in range(BLOCK):
            from_core = (j < ox) == even_a

            @pl.when(from_core)
            def _():
                model[f, j, BLOCK : 2 * BLOCK] = c_ref[f * BLOCK + j]

            @pl.when(jnp.logical_not(from_core))
            def _():
                model[f, j, BLOCK : 2 * BLOCK] = x_ref[f * BLOCK + j]

    field[0:4] = jnp.zeros((4, 48, NZ), F32)
    field[36:40] = jnp.zeros((4, 48, NZ), F32)
    bx[0:4] = jnp.zeros((4, APER, NZ), F32)
    bx[36:40] = jnp.zeros((4, APER, NZ), F32)

    def prepare(i, carry):
        slot = lax.rem(ox + i, APER)
        speed = model[0, slot, pl.ds(oy, APER)]
        dense = model[1, slot, pl.ds(oy, APER)]
        dens[i] = dense
        kap[i] = 0.1 * dense * speed * speed
        buoy[i] = 0.1 / dense
        field[4 + i, 0:8] = jnp.zeros((8, NZ), F32)
        field[4 + i, 40:48] = jnp.zeros((8, NZ), F32)
        by[i, 0:8] = jnp.zeros((8, NZ), F32)
        by[i, 40:48] = jnp.zeros((8, NZ), F32)
        field[4 + i, 8:40] = p0_ref[i]
        for f in range(2):
            terms[f, i] = jnp.zeros((48, NZ), F32)
        return carry

    lax.fori_loop(0, APER, prepare, 0, unroll=2)

    def plus(i0, visit):
        rows = pl.ds(i0, ROWS)
        inner = pl.ds(4 + i0, ROWS)
        gz_all = along_depth(field[inner, 8:40], dplus_mat[...])
        for c in range(4):
            window = field[pl.ds(i0 + 1, ROWS + 7), 8 + 8 * c : 16 + 8 * c]
            gx = stencil(lambda k: window[k : k + ROWS], ROWS)
            gy = stencil(lambda k: field[inner, 5 + 8 * c + k : 13 + 8 * c + k], ROWS)
            visit(rows, c, (gx, gy, gz_all[:, 8 * c : 8 * c + 8]))

    def minus(i0, visit):
        rows = pl.ds(i0, ROWS)
        sz_all = along_depth(bz[rows], dminus_mat[...])
        for c in range(4):
            window = bx[pl.ds(i0, ROWS + 7), 8 * c : 8 * c + 8]
            sx = stencil(lambda k: window[k : k + ROWS], ROWS)
            sy = stencil(lambda k: by[rows, 4 + 8 * c + k : 12 + 8 * c + k], ROWS)
            visit(i0, rows, c, sx + sy + sz_all[:, 8 * c : 8 * c + 8])

    def scaled(rows, c, i0, values):
        cols = slice(8 * c, 8 * c + 8)
        light = buoy[rows, cols]
        bx[pl.ds(4 + i0, ROWS), cols] = light * values[0]
        by[rows, 8 + 8 * c : 16 + 8 * c] = light * values[1]
        bz[rows, cols] = light * values[2]

    def spike(i0, c, weight):
        if c != 2:
            return None
        row = lax.broadcasted_iota(jnp.int32, (ROWS, 8, NZ), 0) + i0
        col = lax.broadcasted_iota(jnp.int32, (ROWS, 8, NZ), 1)
        lane = lax.broadcasted_iota(jnp.int32, (ROWS, 8, NZ), 2)
        return jnp.where((row == 16) & (col == 0) & (lane == 64), weight, 0.0)

    def loop(body):
        lax.fori_loop(0, APER // ROWS, lambda k, carry: (body(k * ROWS), carry)[1], 0)

    def first_plus(i0):
        def visit(rows, c, g):
            cols = slice(8 * c, 8 * c + 8)
            for k in range(3):
                g1[k, rows, cols] = g[k]
            scaled(rows, c, i0, g)

        plus(i0, visit)

    loop(first_plus)

    def first_minus(i0):
        def visit(i0, rows, c, spread):
            cols = slice(8 * c, 8 * c + 8)
            a1[rows, cols] = spread
            place = (pl.ds(4 + i0, ROWS), slice(8 + 8 * c, 16 + 8 * c))
            value = field[place] + kap[rows, cols] * spread
            hit = spike(i0, c, wavelet[0])
            field[place] = value if hit is None else value + hit

        minus(i0, visit)

    loop(first_minus)

    def second_plus(i0):
        def visit(rows, c, g):
            cols = slice(8 * c, 8 * c + 8)
            both = [g1[k, rows, cols] + g[k] for k in range(3)]
            for k in range(3):
                gs[k, rows, cols] = both[k]
            scaled(rows, c, i0, both)

        plus(i0, visit)

    loop(second_plus)

    def second_minus(i0):
        def visit(i0, rows, c, spread):
            cols = slice(8 * c, 8 * c + 8)
            a2[rows, cols] = spread
            place = (pl.ds(4 + i0, ROWS), slice(8 + 8 * c, 16 + 8 * c))
            stiff = kap[rows, cols]
            value = field[place] + stiff * spread
            hit = spike(i0, c, wavelet[1])
            value = value if hit is None else value + hit
            value = value - obs_ref[rows, cols]
            lam[rows, cols] = value
            field[place] = stiff * value

        minus(i0, visit)

    loop(second_minus)

    def third_plus(i0):
        def visit(rows, c, h):
            cols = slice(8 * c, 8 * c + 8)
            quad[rows, cols] = h[0] * gs[0, rows, cols] + h[1] * gs[1, rows, cols] + h[2] * gs[2, rows, cols]
            scaled(rows, c, i0, h)

        plus(i0, visit)

    loop(third_plus)

    def third_minus(i0):
        def visit(i0, rows, c, spread):
            cols = slice(8 * c, 8 * c + 8)
            late = lam[rows, cols]
            early = late + spread
            place = (pl.ds(4 + i0, ROWS), slice(8 + 8 * c, 16 + 8 * c))
            field[place] = kap[rows, cols] * early
            lam[rows, cols] = late * a2[rows, cols] + early * a1[rows, cols]

        minus(i0, visit)

    loop(third_minus)

    def last_plus(i0):
        def visit(rows, c, h):
            cols = slice(8 * c, 8 * c + 8)
            quad[rows, cols] += h[0] * g1[0, rows, cols] + h[1] * g1[1, rows, cols] + h[2] * g1[2, rows, cols]

        plus(i0, visit)

    loop(last_plus)

    def finish(i, carry):
        slot = lax.rem(ox + i, APER)
        speed = model[0, slot, pl.ds(oy, APER)]
        dense = dens[i]
        light = buoy[i]
        stiff = lam[i]
        terms[0, slot, pl.ds(oy, APER)] = 0.2 * dense * speed * stiff
        terms[1, slot, pl.ds(oy, APER)] = 0.1 * speed * speed * stiff + 10.0 * light * light * quad[i]
        return carry

    lax.fori_loop(0, APER, finish, 0, unroll=2)

    for f in range(2):
        rows = slice(f * BLOCK, (f + 1) * BLOCK)
        eh_ref[rows] = terms[f, :BLOCK, pl.ds(col_e, BLOCK)]
        oh_ref[rows] = terms[f, :BLOCK, pl.ds(col_o, BLOCK)]
        ew_ref[rows] = terms[f, BLOCK:, pl.ds(col_e, BLOCK)]
        ow_ref[rows] = terms[f, BLOCK:, pl.ds(col_o, BLOCK)]
        mh_ref[rows] = terms[f, :BLOCK, BLOCK : 2 * BLOCK]
        mw_ref[rows] = terms[f, BLOCK:, BLOCK : 2 * BLOCK]


def wave(corners, p0, obs, own, c, x, ye, yo, ye2, yo2):
    part = jax.ShapeDtypeStruct((2 * BLOCK, BLOCK, NZ), F32)
    cube = pltpu.VMEM((APER, APER, NZ), F32)
    return pl.pallas_call(
        wave_kernel,
        out_shape=(part,) * 6,
        in_specs=[pl.BlockSpec(memory_space=pltpu.SMEM)] + vmem(9),
        out_specs=tuple(vmem(6)),
        scratch_shapes=[
            pltpu.VMEM((2, APER, 48, NZ), F32),
            pltpu.VMEM((2, APER, 48, NZ), F32),
            pltpu.VMEM((APER + 8, 48, NZ), F32),
            pltpu.VMEM((APER + 8, APER, NZ), F32),
            pltpu.VMEM((APER, 48, NZ), F32),
            cube,
            pltpu.VMEM((3, APER, APER, NZ), F32),
            pltpu.VMEM((3, APER, APER, NZ), F32),
            cube, cube, cube, cube, cube, cube, cube,
            pltpu.VMEM((2 * NZ, NZ), jnp.bfloat16),
            pltpu.VMEM((2 * NZ, NZ), jnp.bfloat16),
        ],
        compiler_params=pltpu.CompilerParams(vmem_limit_bytes=32 << 20),
        name="wave",
    )(corners, p0, obs, own, c, x, ye, yo, ye2, yo2)


def combine_kernel(corner_ref, own_ref, e_ref, o_ref, ye_ref, yo_ref, c_ref, x_ref):
    ox = offset_in_frame(corner_ref, 0, "line").astype(F32)
    even = lax.rem(lax.axis_index("line"), 2) == 0
    sign = jnp.where(even, 1.0, -1.0).astype(F32)
    shifts = (jnp.full((BLOCK, NZ), ox, F32), ye_ref[0], yo_ref[0])
    for j in range(BLOCK):
        to_core = [(shift - (j + 0.5)) * sign > 0.0 for shift in shifts]
        for f in range(2):
            r = f * BLOCK + j
            values = (own_ref[r], e_ref[r], o_ref[r])
            near = [jnp.where(m, v, 0.0) for m, v in zip(to_core, values)]
            far = [jnp.where(m, 0.0, v) for m, v in zip(to_core, values)]
            c_ref[r] = near[0] + near[1] + near[2]
            x_ref[r] = far[0] + far[1] + far[2]


def combine(corners, own, e, o, ye, yo):
    part = jax.ShapeDtypeStruct((2 * BLOCK, BLOCK, NZ), F32)
    whole = pl.BlockSpec((2 * BLOCK, BLOCK, NZ), lambda i: (0, 0, 0))
    last = pl.BlockSpec((1, BLOCK, NZ), lambda i: (2 * BLOCK, 0, 0))
    return pl.pallas_call(
        combine_kernel,
        grid=(1,),
        out_shape=(part, part),
        in_specs=[pl.BlockSpec(memory_space=pltpu.SMEM), whole, whole, whole, last, last],
        out_specs=(whole, whole),
        name="combine",
    )(corners, own, e, o, ye, yo)


def total_kernel(own_ref, e_ref, o_ref, c_ref, x_ref, vel_ref, rho_ref):
    for f, out_ref in ((0, vel_ref), (1, rho_ref)):
        rows = slice(f * BLOCK, (f + 1) * BLOCK)
        out_ref[...] = ((own_ref[rows] + e_ref[rows]) + (o_ref[rows] + c_ref[rows])) + x_ref[rows]


def total(*parts):
    block = jax.ShapeDtypeStruct((BLOCK, BLOCK, NZ), F32)
    return pl.pallas_call(
        total_kernel,
        out_shape=(block, block),
        in_specs=vmem(5),
        out_specs=tuple(vmem(2)),
        name="total",
    )(*parts)


def body(velocity, density, start_pressure, observed, corners):
    own = pack(corners, velocity, density)
    x = swap(own, "line", True)
    ye = swap(own, "shot", False)
    yo = swap(own, "shot", True)
    c = swap(own, "line", False)
    ye2, yo2 = relay(c, x, ye, yo)
    ye2 = swap(ye2, "shot", False)
    yo2 = swap(yo2, "shot", True)
    eh, oh, ew, ow, mh, mw = wave(corners, start_pressure, observed, own, c, x, ye, yo, ye2, yo2)
    eh = swap(eh, "shot", False)
    oh = swap(oh, "shot", True)
    ew = swap(ew, "shot", False)
    ow = swap(ow, "shot", True)
    to_core, to_chip = combine(corners, mh, eh, oh, ye, yo)
    chip = swap(to_chip, "line", True)
    core = swap(to_core, "line", False)
    return total(mw, ew, ow, core, chip)


def solution(mesh):
    placed = (P("line", "shot", None),) * 5
    return jax.shard_map(
        body,
        mesh=mesh,
        in_specs=placed,
        out_specs=(P("line", "shot", None),) * 2,
        check_vma=False,
    )
```

```python
import jax
import jax.numpy as jnp
from jax import lax
from jax.experimental import pallas as pl
from jax.experimental.pallas import tpu as pltpu
from jax.sharding import PartitionSpec as P

coeffs = (1225.0 / 1024.0, -245.0 / 3072.0, 49.0 / 5120.0, -5.0 / 7168.0)
UNIT = coeffs[0] / 105.0
wavelet = (20.0, -12.0)

BLOCK = 16
APER = 32
NZ = 128
ROWS = 8
EXTRA = 1
F32 = jnp.float32
small = pltpu.CompilerParams(vmem_limit_bytes=4 << 20)


def swap_pairs(odd):
    pairs = []
    for i in range(1 if odd else 0, 15, 2):
        pairs += [(i, i + 1), (i + 1, i)]
    return pairs


def swap(block, axis, odd):
    return lax.ppermute(block, axis, swap_pairs(odd))


def vmem(count):
    return [pl.BlockSpec(memory_space=pltpu.VMEM)] * count


def offset_in_frame(corner_ref, dim, axis):
    return corner_ref[dim, 0] - (lax.axis_index(axis) - 1) * BLOCK


def side(axis, odd):
    even = lax.rem(lax.axis_index(axis), 2) == 0
    return pl.multiple_of(jnp.where(even, 0, 2 * BLOCK) if odd else jnp.where(even, 2 * BLOCK, 0), BLOCK)


def stencil(window):
    rows = window.shape[0] - 7
    total = None
    for m in range(1, 5):
        part = coeffs[m - 1] * (window[3 + m : 3 + m + rows] - window[4 - m : 4 - m + rows])
        total = part if total is None else total + part
    return total


def band(size, run, first, source_dim):
    source = lax.broadcasted_iota(jnp.int32, (size, size), source_dim)
    target = lax.broadcasted_iota(jnp.int32, (size, size), 1 - source_dim)
    away = source - target + first
    total = jnp.zeros((size, size), F32)
    for m in range(1, 5):
        value = coeffs[m - 1] / UNIT
        total = jnp.where(away == m, value, total)
        total = jnp.where(away == 1 - m, -value, total)
    return jnp.where(source // run == target // run, total, 0.0)


def halves(values):
    flat = values.reshape(-1, NZ)
    upper = flat.astype(jnp.bfloat16)
    lower = (flat - upper.astype(F32)).astype(jnp.bfloat16)
    return jnp.concatenate([upper, lower], axis=1)


def along_depth(both, matrix):
    return jnp.dot(both, matrix, preferred_element_type=F32).reshape(ROWS, APER, NZ)


def along_width(both, matrix):
    out = jnp.dot(matrix, both, preferred_element_type=F32)
    return (out[:, :NZ] + out[:, NZ:]).reshape(ROWS, APER, NZ)


def chunks():
    return range(0, APER, ROWS)


def plus_all(field, i0, wide, deep):
    both = halves(field[4 + i0 : 4 + i0 + ROWS])
    return (
        stencil(field[1 + i0 : 8 + i0 + ROWS]),
        along_width(both, wide),
        along_depth(both, deep),
    )


def early_kernel(corner_ref, p0_ref, obs_ref, field, g1, wide, deep, obs_out, corner_out):
    obs_out[...] = obs_ref[...]
    row = lax.broadcasted_iota(jnp.int32, (8, NZ), 0)
    corner_out[...] = jnp.where(row == 0, corner_ref[0, 0, 0], corner_ref[0, 0, 1])
    for first in range(2):
        wide[first] = band(ROWS * APER, APER, first, 1).astype(jnp.bfloat16)
        half = band(NZ, NZ, first, 0).astype(jnp.bfloat16)
        deep[first] = jnp.concatenate([half, half], axis=0)
    field[0:4] = jnp.zeros((4, APER, NZ), F32)
    field[36:40] = jnp.zeros((4, APER, NZ), F32)
    field[4:36] = p0_ref[...]
    for i0 in chunks():
        for k, g in enumerate(plus_all(field, i0, wide[0], deep[0])):
            g1[k, i0 : i0 + ROWS] = g


def early(corners, p0, obs):
    return pl.pallas_call(
        early_kernel,
        out_shape=(
            jax.ShapeDtypeStruct((APER + 8, APER, NZ), F32),
            jax.ShapeDtypeStruct((3, APER, APER, NZ), F32),
            jax.ShapeDtypeStruct((2, ROWS * APER, ROWS * APER), jnp.bfloat16),
            jax.ShapeDtypeStruct((2, 2 * NZ, NZ), jnp.bfloat16),
            jax.ShapeDtypeStruct((APER, APER, NZ), F32),
            jax.ShapeDtypeStruct((8, NZ), jnp.int32),
        ),
        in_specs=[pl.BlockSpec(memory_space=pltpu.SMEM)] + vmem(2),
        out_specs=tuple(vmem(6)),
        compiler_params=pltpu.CompilerParams(vmem_limit_bytes=8 << 20),
        name="early",
    )(corners, p0, obs)


def wave_kernel(
    field0, g1, wide, deep, obs_ref, corner_vmem, own_ref, ye_ref, yo_ref, x_ref, c_ref, ye2_ref, yo2_ref, cye_ref, cyo_ref,
    c_out, xe_out, xo_out, xm_out, oe_out, oo_out, om_out,
    corner_ref, sem, model, terms, field, bx, by, bz, gs, a1, a2, lam, kap, buoy, quad,
):
    corner_copy = pltpu.make_async_copy(corner_vmem, corner_ref, sem)
    corner_copy.start()
    row_c, row_x = side("line", False), side("line", True)
    col_e, col_o = side("shot", False), side("shot", True)
    middle = slice(BLOCK, 2 * BLOCK)

    for f in range(2):
        rows = slice(f * BLOCK, (f + 1) * BLOCK)
        model[f, middle, middle] = own_ref[rows]
        model[f, middle, pl.ds(col_e, BLOCK)] = ye_ref[rows]
        model[f, middle, pl.ds(col_o, BLOCK)] = yo_ref[rows]
        model[f, pl.ds(row_c, BLOCK), middle] = c_ref[rows]
        model[f, pl.ds(row_c, BLOCK), pl.ds(col_e, BLOCK)] = cye_ref[rows]
        model[f, pl.ds(row_c, BLOCK), pl.ds(col_o, BLOCK)] = cyo_ref[rows]
        model[f, pl.ds(row_x, BLOCK), middle] = x_ref[rows]
        model[f, pl.ds(row_x, BLOCK), pl.ds(col_e, BLOCK)] = ye2_ref[rows]
        model[f, pl.ds(row_x, BLOCK), pl.ds(col_o, BLOCK)] = yo2_ref[rows]
        terms[f] = jnp.zeros((48, 48, NZ), F32)

    for padded in (field, bx):
        padded[0:4] = jnp.zeros((4, APER, NZ), F32)
        padded[36:40] = jnp.zeros((4, APER, NZ), F32)

    corner_copy.wait()
    ox = offset_in_frame(corner_ref, 0, "line")
    oy = offset_in_frame(corner_ref, 1, "shot")

    def scaled(i0, values):
        rows = slice(i0, i0 + ROWS)
        light = buoy[rows]
        bx[4 + i0 : 4 + i0 + ROWS] = light * values[0]
        light = light * (UNIT * UNIT)
        by[rows] = light * values[1]
        bz[rows] = light * values[2]

    def minus(i0):
        rows = slice(i0, i0 + ROWS)
        spread = along_width(halves(by[rows]), wide[1]) + along_depth(halves(bz[rows]), deep[1])
        return spread + stencil(bx[i0 : i0 + ROWS + 7])

    def dotted(h, g):
        return h[0] * g[0] + (UNIT * UNIT) * (h[1] * g[1] + h[2] * g[2])

    row = lax.broadcasted_iota(jnp.int32, (8, NZ), 0)
    lane = lax.broadcasted_iota(jnp.int32, (8, NZ), 1)
    centre = jnp.where((row == 0) & (lane == 64), 1.0, 0.0)

    for i0 in chunks():
        rows = slice(i0, i0 + ROWS)
        for i in range(i0, i0 + ROWS):
            slot = ox + i
            speed = model[0, slot, pl.ds(oy, APER)]
            dense = model[1, slot, pl.ds(oy, APER)]
            kap[i] = 0.1 * dense * speed * speed
            buoy[i] = 0.1 / dense
        scaled(i0, [g1[k, rows] for k in range(3)])

    for i0 in chunks():
        rows = slice(i0, i0 + ROWS)
        inner = slice(4 + i0, 4 + i0 + ROWS)
        spread = minus(i0)
        a1[rows] = spread
        field[inner] = field0[inner] + kap[rows] * spread
    field[20, 16:24] += wavelet[0] * centre

    for i0 in chunks():
        rows = slice(i0, i0 + ROWS)
        g = plus_all(field, i0, wide[0], deep[0])
        both = [g1[k, rows] + g[k] for k in range(3)]
        for k in range(3):
            gs[k, rows] = both[k]
        scaled(i0, both)
    field[20, 16:24] += wavelet[1] * centre

    for i0 in chunks():
        rows = slice(i0, i0 + ROWS)
        inner = slice(4 + i0, 4 + i0 + ROWS)
        spread = minus(i0)
        a2[rows] = spread
        stiff = kap[rows]
        value = field[inner] + stiff * spread - obs_ref[rows]
        lam[rows] = value
        field[inner] = stiff * value

    for i0 in chunks():
        rows = slice(i0, i0 + ROWS)
        h = plus_all(field, i0, wide[0], deep[0])
        quad[rows] = dotted(h, [gs[k, rows] for k in range(3)])
        scaled(i0, h)

    for i0 in chunks():
        rows = slice(i0, i0 + ROWS)
        inner = slice(4 + i0, 4 + i0 + ROWS)
        late = lam[rows]
        early = late + minus(i0)
        field[inner] = kap[rows] * early
        lam[rows] = late * a2[rows] + early * a1[rows]

    for i0 in chunks():
        rows = slice(i0, i0 + ROWS)
        h = plus_all(field, i0, wide[0], deep[0])
        quad[rows] += dotted(h, [g1[k, rows] for k in range(3)])
        for i in range(i0, i0 + ROWS):
            slot = ox + i
            speed = model[0, slot, pl.ds(oy, APER)]
            dense = model[1, slot, pl.ds(oy, APER)]
            light = buoy[i]
            stiff = lam[i]
            terms[0, slot, pl.ds(oy, APER)] = 0.2 * dense * speed * stiff
            terms[1, slot, pl.ds(oy, APER)] = 0.1 * speed * speed * stiff + 10.0 * light * light * quad[i]

    for f in range(2):
        rows = slice(f * BLOCK, (f + 1) * BLOCK)
        c_out[rows] = terms[f, pl.ds(row_c, BLOCK)]
        xe_out[rows] = terms[f, pl.ds(row_x, BLOCK), pl.ds(col_e, BLOCK)]
        xo_out[rows] = terms[f, pl.ds(row_x, BLOCK), pl.ds(col_o, BLOCK)]
        xm_out[rows] = terms[f, pl.ds(row_x, BLOCK), middle]
        oe_out[rows] = terms[f, middle, pl.ds(col_e, BLOCK)]
        oo_out[rows] = terms[f, middle, pl.ds(col_o, BLOCK)]
        om_out[rows] = terms[f, middle, middle]


part = jax.ShapeDtypeStruct((2 * BLOCK, BLOCK, NZ), F32)


def wave(begun, *blocks):
    cube = pltpu.VMEM((APER, APER, NZ), F32)
    padded = pltpu.VMEM((APER + 8, APER, NZ), F32)
    return pl.pallas_call(
        wave_kernel,
        out_shape=(jax.ShapeDtypeStruct((2 * BLOCK, 3 * BLOCK, NZ), F32),) + (part,) * 6,
        in_specs=vmem(15),
        out_specs=tuple(vmem(7)),
        scratch_shapes=[
            pltpu.SMEM((8, NZ), jnp.int32),
            pltpu.SemaphoreType.DMA,
            pltpu.VMEM((2, 48, 48, NZ), F32),
            pltpu.VMEM((2, 48, 48, NZ), F32),
            padded, padded, cube, cube,
            pltpu.VMEM((3, APER, APER, NZ), F32),
            cube, cube, cube, cube, cube, cube,
        ],
        compiler_params=pltpu.CompilerParams(vmem_limit_bytes=26 << 20),
        name="wave",
    )(*begun, *blocks)


def onward_kernel(x_ref, c_ref, out_ref):
    del c_ref
    out_ref[...] = x_ref[...]


def onward(x, c):
    return pl.pallas_call(
        onward_kernel,
        out_shape=part,
        in_specs=vmem(1) + [pl.BlockSpec(memory_space=pl.ANY)],
        out_specs=vmem(1)[0],
        compiler_params=small,
        name="onward",
    )(x, c)


def merge_kernel(first_ref, c_ref, oe_ref, oo_ref, om_ref, oe_out, oo_out, om_out):
    del first_ref
    oe_out[...] = oe_ref[...] + c_ref[:, pl.ds(side("shot", False), BLOCK)]
    oo_out[: 2 * BLOCK] = oo_ref[...] + c_ref[:, pl.ds(side("shot", True), BLOCK)]
    oo_out[2 * BLOCK :] = jnp.zeros((EXTRA, BLOCK, NZ), F32)
    om_out[...] = om_ref[...] + c_ref[:, BLOCK : 2 * BLOCK]


def merge(first, c, oe, oo, om):
    return pl.pallas_call(
        merge_kernel,
        out_shape=(part, jax.ShapeDtypeStruct((2 * BLOCK + EXTRA, BLOCK, NZ), F32), part),
        in_specs=[pl.BlockSpec(memory_space=pl.ANY)] + vmem(4),
        out_specs=tuple(vmem(3)),
        compiler_params=small,
        name="merge",
    )(first, c, oe, oo, om)


def combine_kernel(m_ref, e_ref, o_ref, oe_ref, out_ref, oe_out):
    del oe_ref, oe_out
    out_ref[...] = m_ref[...] + e_ref[...] + o_ref[...]


def combine(m, e, o, oe):
    place = pl.BlockSpec(memory_space=pl.ANY)
    return pl.pallas_call(
        combine_kernel,
        out_shape=(part, part),
        in_specs=vmem(3) + [place],
        out_specs=(vmem(1)[0], place),
        input_output_aliases={3: 1},
        compiler_params=small,
        name="combine",
    )(m, e, o, oe)


def total_kernel(own_ref, x_ref, e_ref, o_ref, vel_ref, rho_ref):
    for f, out_ref in ((0, vel_ref), (1, rho_ref)):
        rows = slice(f * BLOCK, (f + 1) * BLOCK)
        out_ref[...] = (own_ref[rows] + x_ref[rows]) + (e_ref[rows] + o_ref[rows])


def total(*parts):
    block = jax.ShapeDtypeStruct((BLOCK, BLOCK, NZ), F32)
    return pl.pallas_call(
        total_kernel,
        out_shape=(block, block),
        in_specs=vmem(4),
        out_specs=tuple(vmem(2)),
        compiler_params=small,
        name="total",
    )(*parts)


def body(velocity, density, start_pressure, observed, corners):
    own = jnp.stack([velocity, density]).reshape(2 * BLOCK, BLOCK, NZ)
    c = swap(own, "line", False)
    x = swap(own, "line", True)
    yo = swap(own, "shot", True)
    ye = swap(own, "shot", False)
    begun = early(corners, start_pressure, observed)
    passed = onward(x, c)
    yo2 = swap(passed, "shot", True)
    ye2 = swap(passed, "shot", False)
    cyo = swap(yo, "line", False)
    cye = swap(ye, "line", False)
    to_core, xe, xo, xm, oe, oo, om = wave(begun, own, ye, yo, x, c, ye2, yo2, cye, cyo)
    to_core = swap(to_core, "line", False)
    xo = swap(xo, "shot", True)
    xe = swap(xe, "shot", False)
    oe, oo, om = merge(xe, to_core, oe, oo, om)
    oo = swap(oo, "shot", True)
    xm, oe = combine(xm, xe, xo, oe)
    xm = swap(xm, "line", True)
    oe = swap(oe, "shot", False)
    return total(om, xm, oe, oo)


def solution(mesh):
    placed = (P("line", "shot", None),) * 5
    return jax.shard_map(
        body,
        mesh=mesh,
        in_specs=placed,
        out_specs=(P("line", "shot", None),) * 2,
        check_vma=False,
    )
```

```python
import jax
import jax.numpy as jnp
from jax import lax
from jax.experimental import pallas as pl
from jax.experimental.pallas import tpu as pltpu
from jax.sharding import PartitionSpec as P

coeffs = (1225.0 / 1024.0, -245.0 / 3072.0, 49.0 / 5120.0, -5.0 / 7168.0)
UNIT = coeffs[0] / 105.0
wavelet = (20.0, -12.0)

BLOCK = 16
APER = 32
NZ = 128
ROWS = 8
EXTRA = 1
F32 = jnp.float32
small = pltpu.CompilerParams(vmem_limit_bytes=4 << 20)


def swap_pairs(odd):
    pairs = []
    for i in range(1 if odd else 0, 15, 2):
        pairs += [(i, i + 1), (i + 1, i)]
    return pairs


def swap(block, axis, odd):
    return lax.ppermute(block, axis, swap_pairs(odd))


def vmem(count):
    return [pl.BlockSpec(memory_space=pltpu.VMEM)] * count


def offset_in_frame(corner_ref, dim, axis):
    return corner_ref[dim, 0] - (lax.axis_index(axis) - 1) * BLOCK


def side(axis, odd):
    even = lax.rem(lax.axis_index(axis), 2) == 0
    return pl.multiple_of(jnp.where(even, 0, 2 * BLOCK) if odd else jnp.where(even, 2 * BLOCK, 0), BLOCK)


def stencil(window):
    rows = window.shape[0] - 7
    total = None
    for m in range(1, 5):
        part = coeffs[m - 1] * (window[3 + m : 3 + m + rows] - window[4 - m : 4 - m + rows])
        total = part if total is None else total + part
    return total


def band(size, run, first, source_dim):
    source = lax.broadcasted_iota(jnp.int32, (size, size), source_dim)
    target = lax.broadcasted_iota(jnp.int32, (size, size), 1 - source_dim)
    away = source - target + first
    total = jnp.zeros((size, size), F32)
    for m in range(1, 5):
        value = coeffs[m - 1] / UNIT
        total = jnp.where(away == m, value, total)
        total = jnp.where(away == 1 - m, -value, total)
    return jnp.where(source // run == target // run, total, 0.0)


def halves(values):
    flat = values.reshape(-1, NZ)
    upper = flat.astype(jnp.bfloat16)
    lower = (flat - upper.astype(F32)).astype(jnp.bfloat16)
    return jnp.concatenate([upper, lower], axis=1)


def along_depth(both, matrix):
    return jnp.dot(both, matrix, preferred_element_type=F32).reshape(ROWS, APER, NZ)


def along_width(both, matrix):
    out = jnp.dot(matrix, both, preferred_element_type=F32)
    return (out[:, :NZ] + out[:, NZ:]).reshape(ROWS, APER, NZ)


def chunks():
    return range(0, APER, ROWS)


def plus_all(field, i0, wide, deep):
    both = halves(field[4 + i0 : 4 + i0 + ROWS])
    return (
        stencil(field[1 + i0 : 8 + i0 + ROWS]),
        along_width(both, wide),
        along_depth(both, deep),
    )


def early_kernel(corner_ref, p0_ref, obs_ref, field, g1, wide, deep, obs_out, corner_out):
    obs_out[...] = obs_ref[...]
    row = lax.broadcasted_iota(jnp.int32, (8, NZ), 0)
    corner_out[...] = jnp.where(row == 0, corner_ref[0, 0, 0], corner_ref[0, 0, 1])
    for first in range(2):
        wide[first] = band(ROWS * APER, APER, first, 1).astype(jnp.bfloat16)
        half = band(NZ, NZ, first, 0).astype(jnp.bfloat16)
        deep[first] = jnp.concatenate([half, half], axis=0)
    field[0:4] = jnp.zeros((4, APER, NZ), F32)
    field[36:40] = jnp.zeros((4, APER, NZ), F32)
    field[4:36] = p0_ref[...]
    for i0 in chunks():
        for k, g in enumerate(plus_all(field, i0, wide[0], deep[0])):
            g1[k, i0 : i0 + ROWS] = g


def early(corners, p0, obs):
    return pl.pallas_call(
        early_kernel,
        out_shape=(
            jax.ShapeDtypeStruct((APER + 8, APER, NZ), F32),
            jax.ShapeDtypeStruct((3, APER, APER, NZ), F32),
            jax.ShapeDtypeStruct((2, ROWS * APER, ROWS * APER), jnp.bfloat16),
            jax.ShapeDtypeStruct((2, 2 * NZ, NZ), jnp.bfloat16),
            jax.ShapeDtypeStruct((APER, APER, NZ), F32),
            jax.ShapeDtypeStruct((8, NZ), jnp.int32),
        ),
        in_specs=[pl.BlockSpec(memory_space=pltpu.SMEM)] + vmem(2),
        out_specs=tuple(vmem(6)),
        compiler_params=pltpu.CompilerParams(vmem_limit_bytes=8 << 20),
        name="early",
    )(corners, p0, obs)


def wave_kernel(
    field0, g1, wide, deep, obs_ref, corner_vmem, own_ref, ye_ref, yo_ref, x_ref, c_ref, ye2_ref, yo2_ref, cye_ref, cyo_ref,
    ce_out, co_out, cm_out, xe_out, xo_out, xm_out, oe_out, oo_out, om_out,
    corner_ref, sem, model, terms, field, bx, by, bz, gs, a1, a2, lam, kap, buoy, quad,
):
    corner_copy = pltpu.make_async_copy(corner_vmem, corner_ref, sem)
    corner_copy.start()
    row_c, row_x = side("line", False), side("line", True)
    col_e, col_o = side("shot", False), side("shot", True)
    middle = slice(BLOCK, 2 * BLOCK)

    for f in range(2):
        rows = slice(f * BLOCK, (f + 1) * BLOCK)
        model[f, middle, middle] = own_ref[rows]
        model[f, middle, pl.ds(col_e, BLOCK)] = ye_ref[rows]
        model[f, middle, pl.ds(col_o, BLOCK)] = yo_ref[rows]
        model[f, pl.ds(row_c, BLOCK), middle] = c_ref[rows]
        model[f, pl.ds(row_c, BLOCK), pl.ds(col_e, BLOCK)] = cye_ref[rows]
        model[f, pl.ds(row_c, BLOCK), pl.ds(col_o, BLOCK)] = cyo_ref[rows]
        model[f, pl.ds(row_x, BLOCK), middle] = x_ref[rows]
        model[f, pl.ds(row_x, BLOCK), pl.ds(col_e, BLOCK)] = ye2_ref[rows]
        model[f, pl.ds(row_x, BLOCK), pl.ds(col_o, BLOCK)] = yo2_ref[rows]
        terms[f] = jnp.zeros((48, 48, NZ), F32)

    for padded in (field, bx):
        padded[0:4] = jnp.zeros((4, APER, NZ), F32)
        padded[36:40] = jnp.zeros((4, APER, NZ), F32)

    corner_copy.wait()
    ox = offset_in_frame(corner_ref, 0, "line")
    oy = offset_in_frame(corner_ref, 1, "shot")

    def scaled(i0, values):
        rows = slice(i0, i0 + ROWS)
        light = buoy[rows]
        bx[4 + i0 : 4 + i0 + ROWS] = light * values[0]
        light = light * (UNIT * UNIT)
        by[rows] = light * values[1]
        bz[rows] = light * values[2]

    def minus(i0):
        rows = slice(i0, i0 + ROWS)
        spread = along_width(halves(by[rows]), wide[1]) + along_depth(halves(bz[rows]), deep[1])
        return spread + stencil(bx[i0 : i0 + ROWS + 7])

    def dotted(h, g):
        return h[0] * g[0] + (UNIT * UNIT) * (h[1] * g[1] + h[2] * g[2])

    row = lax.broadcasted_iota(jnp.int32, (8, NZ), 0)
    lane = lax.broadcasted_iota(jnp.int32, (8, NZ), 1)
    centre = jnp.where((row == 0) & (lane == 64), 1.0, 0.0)

    for i0 in chunks():
        rows = slice(i0, i0 + ROWS)
        for i in range(i0, i0 + ROWS):
            slot = ox + i
            speed = model[0, slot, pl.ds(oy, APER)]
            dense = model[1, slot, pl.ds(oy, APER)]
            kap[i] = 0.1 * dense * speed * speed
            buoy[i] = 0.1 / dense
        scaled(i0, [g1[k, rows] for k in range(3)])

    for i0 in chunks():
        rows = slice(i0, i0 + ROWS)
        inner = slice(4 + i0, 4 + i0 + ROWS)
        spread = minus(i0)
        a1[rows] = spread
        field[inner] = field0[inner] + kap[rows] * spread
    field[20, 16:24] += wavelet[0] * centre

    for i0 in chunks():
        rows = slice(i0, i0 + ROWS)
        g = plus_all(field, i0, wide[0], deep[0])
        both = [g1[k, rows] + g[k] for k in range(3)]
        for k in range(3):
            gs[k, rows] = both[k]
        scaled(i0, both)
    field[20, 16:24] += wavelet[1] * centre

    for i0 in chunks():
        rows = slice(i0, i0 + ROWS)
        inner = slice(4 + i0, 4 + i0 + ROWS)
        spread = minus(i0)
        a2[rows] = spread
        stiff = kap[rows]
        value = field[inner] + stiff * spread - obs_ref[rows]
        lam[rows] = value
        field[inner] = stiff * value

    for i0 in chunks():
        rows = slice(i0, i0 + ROWS)
        h = plus_all(field, i0, wide[0], deep[0])
        quad[rows] = dotted(h, [gs[k, rows] for k in range(3)])
        scaled(i0, h)

    for i0 in chunks():
        rows = slice(i0, i0 + ROWS)
        inner = slice(4 + i0, 4 + i0 + ROWS)
        late = lam[rows]
        early = late + minus(i0)
        field[inner] = kap[rows] * early
        lam[rows] = late * a2[rows] + early * a1[rows]

    for i0 in chunks():
        rows = slice(i0, i0 + ROWS)
        h = plus_all(field, i0, wide[0], deep[0])
        quad[rows] += dotted(h, [g1[k, rows] for k in range(3)])
        for i in range(i0, i0 + ROWS):
            slot = ox + i
            speed = model[0, slot, pl.ds(oy, APER)]
            dense = model[1, slot, pl.ds(oy, APER)]
            light = buoy[i]
            stiff = lam[i]
            terms[0, slot, pl.ds(oy, APER)] = 0.2 * dense * speed * stiff
            terms[1, slot, pl.ds(oy, APER)] = 0.1 * speed * speed * stiff + 10.0 * light * light * quad[i]

    for f in range(2):
        rows = slice(f * BLOCK, (f + 1) * BLOCK)
        ce_out[rows] = terms[f, pl.ds(row_c, BLOCK), pl.ds(col_e, BLOCK)]
        co_out[rows] = terms[f, pl.ds(row_c, BLOCK), pl.ds(col_o, BLOCK)]
        cm_out[rows] = terms[f, pl.ds(row_c, BLOCK), middle]
        xe_out[rows] = terms[f, pl.ds(row_x, BLOCK), pl.ds(col_e, BLOCK)]
        xo_out[rows] = terms[f, pl.ds(row_x, BLOCK), pl.ds(col_o, BLOCK)]
        xm_out[rows] = terms[f, pl.ds(row_x, BLOCK), middle]
        oe_out[rows] = terms[f, middle, pl.ds(col_e, BLOCK)]
        oo_out[rows] = terms[f, middle, pl.ds(col_o, BLOCK)]
        om_out[rows] = terms[f, middle, middle]
    for out_ref in (xe_out, xo_out):
        out_ref[2 * BLOCK :] = jnp.zeros((2 * EXTRA, BLOCK, NZ), F32)


part = jax.ShapeDtypeStruct((2 * BLOCK, BLOCK, NZ), F32)
early_part = jax.ShapeDtypeStruct((2 * BLOCK + 2 * EXTRA, BLOCK, NZ), F32)


def wave(begun, *blocks):
    cube = pltpu.VMEM((APER, APER, NZ), F32)
    padded = pltpu.VMEM((APER + 8, APER, NZ), F32)
    return pl.pallas_call(
        wave_kernel,
        out_shape=(part,) * 3 + (early_part,) * 2 + (part,) * 4,
        in_specs=vmem(15),
        out_specs=tuple(vmem(9)),
        scratch_shapes=[
            pltpu.SMEM((8, NZ), jnp.int32),
            pltpu.SemaphoreType.DMA,
            pltpu.VMEM((2, 48, 48, NZ), F32),
            pltpu.VMEM((2, 48, 48, NZ), F32),
            padded, padded, cube, cube,
            pltpu.VMEM((3, APER, APER, NZ), F32),
            cube, cube, cube, cube, cube, cube,
        ],
        compiler_params=pltpu.CompilerParams(vmem_limit_bytes=26 << 20),
        name="wave",
    )(*begun, *blocks)


def onward_kernel(x_ref, c_ref, out_ref):
    del c_ref
    out_ref[...] = x_ref[...]


def onward(x, c):
    return pl.pallas_call(
        onward_kernel,
        out_shape=part,
        in_specs=vmem(1) + [pl.BlockSpec(memory_space=pl.ANY)],
        out_specs=vmem(1)[0],
        compiler_params=small,
        name="onward",
    )(x, c)


def merge_kernel(c_ref, o_ref, out_ref):
    out_ref[: 2 * BLOCK] = o_ref[...] + c_ref[...]
    out_ref[2 * BLOCK :] = jnp.zeros((EXTRA, BLOCK, NZ), F32)


def merge(c, o):
    return pl.pallas_call(
        merge_kernel,
        out_shape=jax.ShapeDtypeStruct((2 * BLOCK + EXTRA, BLOCK, NZ), F32),
        in_specs=vmem(2),
        out_specs=vmem(1)[0],
        compiler_params=small,
        name="merge",
    )(c, o)


def combine_kernel(m_ref, e_ref, o_ref, c_ref, oe_ref, out_ref, oe_out):
    out_ref[...] = m_ref[...] + e_ref[: 2 * BLOCK] + o_ref[: 2 * BLOCK]
    oe_out[...] = oe_ref[...] + c_ref[...]


def combine(m, e, o, c, oe):
    return pl.pallas_call(
        combine_kernel,
        out_shape=(part, part),
        in_specs=vmem(5),
        out_specs=tuple(vmem(2)),
        compiler_params=small,
        name="combine",
    )(m, e, o, c, oe)


def total_kernel(own_ref, c_ref, x_ref, e_ref, o_ref, vel_ref, rho_ref):
    for f, out_ref in ((0, vel_ref), (1, rho_ref)):
        rows = slice(f * BLOCK, (f + 1) * BLOCK)
        out_ref[...] = ((own_ref[rows] + c_ref[rows]) + x_ref[rows]) + (e_ref[rows] + o_ref[rows])


def total(*parts):
    block = jax.ShapeDtypeStruct((BLOCK, BLOCK, NZ), F32)
    return pl.pallas_call(
        total_kernel,
        out_shape=(block, block),
        in_specs=vmem(5),
        out_specs=tuple(vmem(2)),
        compiler_params=small,
        name="total",
    )(*parts)


def body(velocity, density, start_pressure, observed, corners):
    own = jnp.stack([velocity, density]).reshape(2 * BLOCK, BLOCK, NZ)
    c = swap(own, "line", False)
    x = swap(own, "line", True)
    yo = swap(own, "shot", True)
    ye = swap(own, "shot", False)
    begun = early(corners, start_pressure, observed)
    passed = onward(x, c)
    yo2 = swap(passed, "shot", True)
    ye2 = swap(passed, "shot", False)
    cyo = swap(yo, "line", False)
    cye = swap(ye, "line", False)
    ce, co, cm, xe, xo, xm, oe, oo, om = wave(begun, own, ye, yo, x, c, ye2, yo2, cye, cyo)
    xo = swap(xo, "shot", True)
    xe = swap(xe, "shot", False)
    ce, co, cm = (swap(block, "line", False) for block in (ce, co, cm))
    oo = swap(merge(co, oo), "shot", True)
    xm, oe = combine(xm, xe, xo, ce, oe)
    xm = swap(xm, "line", True)
    oe = swap(oe, "shot", False)
    return total(om, cm, xm, oe, oo)


def solution(mesh):
    placed = (P("line", "shot", None),) * 5
    return jax.shard_map(
        body,
        mesh=mesh,
        in_specs=placed,
        out_specs=(P("line", "shot", None),) * 2,
        check_vma=False,
    )
```

```python
import jax
import jax.numpy as jnp
from jax import lax
from jax.experimental import pallas as pl
from jax.experimental.pallas import tpu as pltpu
from jax.sharding import PartitionSpec as P

coeffs = (1225.0 / 1024.0, -245.0 / 3072.0, 49.0 / 5120.0, -5.0 / 7168.0)
UNIT = coeffs[0] / 105.0
wavelet = (20.0, -12.0)

BLOCK = 16
APER = 32
NZ = 128
ROWS = 8
EXTRA = 1
F32 = jnp.float32
small = pltpu.CompilerParams(vmem_limit_bytes=4 << 20)


def swap_pairs(odd):
    pairs = []
    for i in range(1 if odd else 0, 15, 2):
        pairs += [(i, i + 1), (i + 1, i)]
    return pairs


def swap(block, axis, odd):
    return lax.ppermute(block, axis, swap_pairs(odd))


def vmem(count):
    return [pl.BlockSpec(memory_space=pltpu.VMEM)] * count


def offset_in_frame(corner_ref, dim, axis):
    return corner_ref[dim, 0] - (lax.axis_index(axis) - 1) * BLOCK


def side(axis, odd):
    even = lax.rem(lax.axis_index(axis), 2) == 0
    return pl.multiple_of(jnp.where(even, 0, 2 * BLOCK) if odd else jnp.where(even, 2 * BLOCK, 0), BLOCK)


def stencil(window):
    rows = window.shape[0] - 7
    total = None
    for m in range(1, 5):
        part = coeffs[m - 1] * (window[3 + m : 3 + m + rows] - window[4 - m : 4 - m + rows])
        total = part if total is None else total + part
    return total


def band(size, run, first, source_dim):
    source = lax.broadcasted_iota(jnp.int32, (size, size), source_dim)
    target = lax.broadcasted_iota(jnp.int32, (size, size), 1 - source_dim)
    away = source - target + first
    total = jnp.zeros((size, size), F32)
    for m in range(1, 5):
        value = coeffs[m - 1] / UNIT
        total = jnp.where(away == m, value, total)
        total = jnp.where(away == 1 - m, -value, total)
    return jnp.where(source // run == target // run, total, 0.0)


def halves(values):
    flat = values.reshape(-1, NZ)
    upper = flat.astype(jnp.bfloat16)
    lower = (flat - upper.astype(F32)).astype(jnp.bfloat16)
    return jnp.concatenate([upper, lower], axis=1)


def along_depth(both, matrix):
    return jnp.dot(both, matrix, preferred_element_type=F32).reshape(ROWS, APER, NZ)


def along_width(both, matrix):
    out = jnp.dot(matrix, both, preferred_element_type=F32)
    return (out[:, :NZ] + out[:, NZ:]).reshape(ROWS, APER, NZ)


def chunks():
    return range(0, APER, ROWS)


def plus_all(field, i0, wide, deep):
    both = halves(field[4 + i0 : 4 + i0 + ROWS])
    return (
        stencil(field[1 + i0 : 8 + i0 + ROWS]),
        along_width(both, wide),
        along_depth(both, deep),
    )


def early_kernel(corner_ref, p0_ref, obs_ref, field, g1, wide, deep, obs_out, corner_out):
    obs_out[...] = obs_ref[...]
    row = lax.broadcasted_iota(jnp.int32, (8, NZ), 0)
    corner_out[...] = jnp.where(row == 0, corner_ref[0, 0, 0], corner_ref[0, 0, 1])
    for first in range(2):
        wide[first] = band(ROWS * APER, APER, first, 1).astype(jnp.bfloat16)
        half = band(NZ, NZ, first, 0).astype(jnp.bfloat16)
        deep[first] = jnp.concatenate([half, half], axis=0)
    field[0:4] = jnp.zeros((4, APER, NZ), F32)
    field[36:40] = jnp.zeros((4, APER, NZ), F32)
    field[4:36] = p0_ref[...]
    for i0 in chunks():
        for k, g in enumerate(plus_all(field, i0, wide[0], deep[0])):
            g1[k, i0 : i0 + ROWS] = g


def early(corners, p0, obs):
    return pl.pallas_call(
        early_kernel,
        out_shape=(
            jax.ShapeDtypeStruct((APER + 8, APER, NZ), F32),
            jax.ShapeDtypeStruct((3, APER, APER, NZ), F32),
            jax.ShapeDtypeStruct((2, ROWS * APER, ROWS * APER), jnp.bfloat16),
            jax.ShapeDtypeStruct((2, 2 * NZ, NZ), jnp.bfloat16),
            jax.ShapeDtypeStruct((APER, APER, NZ), F32),
            jax.ShapeDtypeStruct((8, NZ), jnp.int32),
        ),
        in_specs=[pl.BlockSpec(memory_space=pltpu.SMEM)] + vmem(2),
        out_specs=tuple(vmem(6)),
        compiler_params=pltpu.CompilerParams(vmem_limit_bytes=8 << 20),
        name="early",
    )(corners, p0, obs)


def wave_kernel(
    field0, g1, wide, deep, obs_ref, corner_vmem, own_ref, ye_ref, yo_ref, c_ref, x_ref, ye2_ref, yo2_ref, cye_ref, cyo_ref,
    ce_out, co_out, cm_out, xe_out, xo_out, xm_out, oe_out, oo_out, om_out,
    corner_ref, sem, model, terms, field, bx, by, bz, gs, a1, a2, lam, kap, buoy, quad,
):
    corner_copy = pltpu.make_async_copy(corner_vmem, corner_ref, sem)
    corner_copy.start()
    row_c, row_x = side("line", False), side("line", True)
    col_e, col_o = side("shot", False), side("shot", True)
    middle = slice(BLOCK, 2 * BLOCK)

    for f in range(2):
        rows = slice(f * BLOCK, (f + 1) * BLOCK)
        model[f, middle, middle] = own_ref[rows]
        model[f, middle, pl.ds(col_e, BLOCK)] = ye_ref[rows]
        model[f, middle, pl.ds(col_o, BLOCK)] = yo_ref[rows]
        model[f, pl.ds(row_c, BLOCK), middle] = c_ref[rows]
        model[f, pl.ds(row_c, BLOCK), pl.ds(col_e, BLOCK)] = cye_ref[rows]
        model[f, pl.ds(row_c, BLOCK), pl.ds(col_o, BLOCK)] = cyo_ref[rows]
        model[f, pl.ds(row_x, BLOCK), middle] = x_ref[rows]
        model[f, pl.ds(row_x, BLOCK), pl.ds(col_e, BLOCK)] = ye2_ref[rows]
        model[f, pl.ds(row_x, BLOCK), pl.ds(col_o, BLOCK)] = yo2_ref[rows]
        terms[f] = jnp.zeros((48, 48, NZ), F32)

    for padded in (field, bx):
        padded[0:4] = jnp.zeros((4, APER, NZ), F32)
        padded[36:40] = jnp.zeros((4, APER, NZ), F32)

    corner_copy.wait()
    ox = offset_in_frame(corner_ref, 0, "line")
    oy = offset_in_frame(corner_ref, 1, "shot")

    def scaled(i0, values):
        rows = slice(i0, i0 + ROWS)
        light = buoy[rows]
        bx[4 + i0 : 4 + i0 + ROWS] = light * values[0]
        light = light * (UNIT * UNIT)
        by[rows] = light * values[1]
        bz[rows] = light * values[2]

    def minus(i0):
        rows = slice(i0, i0 + ROWS)
        spread = along_width(halves(by[rows]), wide[1]) + along_depth(halves(bz[rows]), deep[1])
        return spread + stencil(bx[i0 : i0 + ROWS + 7])

    def dotted(h, g):
        return h[0] * g[0] + (UNIT * UNIT) * (h[1] * g[1] + h[2] * g[2])

    row = lax.broadcasted_iota(jnp.int32, (8, NZ), 0)
    lane = lax.broadcasted_iota(jnp.int32, (8, NZ), 1)
    centre = jnp.where((row == 0) & (lane == 64), 1.0, 0.0)

    for i0 in chunks():
        rows = slice(i0, i0 + ROWS)
        for i in range(i0, i0 + ROWS):
            slot = ox + i
            speed = model[0, slot, pl.ds(oy, APER)]
            dense = model[1, slot, pl.ds(oy, APER)]
            kap[i] = 0.1 * dense * speed * speed
            buoy[i] = 0.1 / dense
        scaled(i0, [g1[k, rows] for k in range(3)])

    for i0 in chunks():
        rows = slice(i0, i0 + ROWS)
        inner = slice(4 + i0, 4 + i0 + ROWS)
        spread = minus(i0)
        a1[rows] = spread
        field[inner] = field0[inner] + kap[rows] * spread
    field[20, 16:24] += wavelet[0] * centre

    for i0 in chunks():
        rows = slice(i0, i0 + ROWS)
        g = plus_all(field, i0, wide[0], deep[0])
        both = [g1[k, rows] + g[k] for k in range(3)]
        for k in range(3):
            gs[k, rows] = both[k]
        scaled(i0, both)
    field[20, 16:24] += wavelet[1] * centre

    for i0 in chunks():
        rows = slice(i0, i0 + ROWS)
        inner = slice(4 + i0, 4 + i0 + ROWS)
        spread = minus(i0)
        a2[rows] = spread
        stiff = kap[rows]
        value = field[inner] + stiff * spread - obs_ref[rows]
        lam[rows] = value
        field[inner] = stiff * value

    for i0 in chunks():
        rows = slice(i0, i0 + ROWS)
        h = plus_all(field, i0, wide[0], deep[0])
        quad[rows] = dotted(h, [gs[k, rows] for k in range(3)])
        scaled(i0, h)

    for i0 in chunks():
        rows = slice(i0, i0 + ROWS)
        inner = slice(4 + i0, 4 + i0 + ROWS)
        late = lam[rows]
        early = late + minus(i0)
        field[inner] = kap[rows] * early
        lam[rows] = late * a2[rows] + early * a1[rows]

    for i0 in chunks():
        rows = slice(i0, i0 + ROWS)
        h = plus_all(field, i0, wide[0], deep[0])
        quad[rows] += dotted(h, [g1[k, rows] for k in range(3)])
        for i in range(i0, i0 + ROWS):
            slot = ox + i
            speed = model[0, slot, pl.ds(oy, APER)]
            dense = model[1, slot, pl.ds(oy, APER)]
            light = buoy[i]
            stiff = lam[i]
            terms[0, slot, pl.ds(oy, APER)] = 0.2 * dense * speed * stiff
            terms[1, slot, pl.ds(oy, APER)] = 0.1 * speed * speed * stiff + 10.0 * light * light * quad[i]

    for f in range(2):
        rows = slice(f * BLOCK, (f + 1) * BLOCK)
        ce_out[rows] = terms[f, pl.ds(row_c, BLOCK), pl.ds(col_e, BLOCK)]
        co_out[rows] = terms[f, pl.ds(row_c, BLOCK), pl.ds(col_o, BLOCK)]
        cm_out[rows] = terms[f, pl.ds(row_c, BLOCK), middle]
        xe_out[rows] = terms[f, pl.ds(row_x, BLOCK), pl.ds(col_e, BLOCK)]
        xo_out[rows] = terms[f, pl.ds(row_x, BLOCK), pl.ds(col_o, BLOCK)]
        xm_out[rows] = terms[f, pl.ds(row_x, BLOCK), middle]
        oe_out[rows] = terms[f, middle, pl.ds(col_e, BLOCK)]
        oo_out[rows] = terms[f, middle, pl.ds(col_o, BLOCK)]
        om_out[rows] = terms[f, middle, middle]
    for out_ref in (xe_out, xo_out):
        out_ref[2 * BLOCK :] = jnp.zeros((2 * EXTRA, BLOCK, NZ), F32)


part = jax.ShapeDtypeStruct((2 * BLOCK, BLOCK, NZ), F32)
early_part = jax.ShapeDtypeStruct((2 * BLOCK + 2 * EXTRA, BLOCK, NZ), F32)


def wave(begun, *blocks):
    cube = pltpu.VMEM((APER, APER, NZ), F32)
    padded = pltpu.VMEM((APER + 8, APER, NZ), F32)
    return pl.pallas_call(
        wave_kernel,
        out_shape=(part,) * 3 + (early_part,) * 2 + (part,) * 4,
        in_specs=vmem(15),
        out_specs=tuple(vmem(9)),
        scratch_shapes=[
            pltpu.SMEM((8, NZ), jnp.int32),
            pltpu.SemaphoreType.DMA,
            pltpu.VMEM((2, 48, 48, NZ), F32),
            pltpu.VMEM((2, 48, 48, NZ), F32),
            padded, padded, cube, cube,
            pltpu.VMEM((3, APER, APER, NZ), F32),
            cube, cube, cube, cube, cube, cube,
        ],
        compiler_params=pltpu.CompilerParams(vmem_limit_bytes=26 << 20),
        name="wave",
    )(*begun, *blocks)


def onward_kernel(x_ref, c_ref, out_ref):
    del c_ref
    out_ref[...] = x_ref[...]


def onward(x, c):
    return pl.pallas_call(
        onward_kernel,
        out_shape=part,
        in_specs=vmem(1) + [pl.BlockSpec(memory_space=pl.ANY)],
        out_specs=vmem(1)[0],
        compiler_params=small,
        name="onward",
    )(x, c)


def merge_kernel(c_ref, o_ref, out_ref):
    out_ref[: 2 * BLOCK] = o_ref[...] + c_ref[...]
    out_ref[2 * BLOCK :] = jnp.zeros((EXTRA, BLOCK, NZ), F32)


def merge(c, o):
    return pl.pallas_call(
        merge_kernel,
        out_shape=jax.ShapeDtypeStruct((2 * BLOCK + EXTRA, BLOCK, NZ), F32),
        in_specs=vmem(2),
        out_specs=vmem(1)[0],
        compiler_params=small,
        name="merge",
    )(c, o)


def combine_kernel(m_ref, e_ref, o_ref, c_ref, oe_ref, out_ref, oe_out):
    out_ref[...] = m_ref[...] + e_ref[: 2 * BLOCK] + o_ref[: 2 * BLOCK]
    oe_out[...] = oe_ref[...] + c_ref[...]


def combine(m, e, o, c, oe):
    return pl.pallas_call(
        combine_kernel,
        out_shape=(part, part),
        in_specs=vmem(5),
        out_specs=tuple(vmem(2)),
        compiler_params=small,
        name="combine",
    )(m, e, o, c, oe)


def total_kernel(own_ref, c_ref, x_ref, e_ref, o_ref, vel_ref, rho_ref):
    for f, out_ref in ((0, vel_ref), (1, rho_ref)):
        rows = slice(f * BLOCK, (f + 1) * BLOCK)
        out_ref[...] = ((own_ref[rows] + c_ref[rows]) + x_ref[rows]) + (e_ref[rows] + o_ref[rows])


def total(*parts):
    block = jax.ShapeDtypeStruct((BLOCK, BLOCK, NZ), F32)
    return pl.pallas_call(
        total_kernel,
        out_shape=(block, block),
        in_specs=vmem(5),
        out_specs=tuple(vmem(2)),
        compiler_params=small,
        name="total",
    )(*parts)


def body(velocity, density, start_pressure, observed, corners):
    own = jnp.stack([velocity, density]).reshape(2 * BLOCK, BLOCK, NZ)
    c = swap(own, "line", False)
    x = swap(own, "line", True)
    yo = swap(own, "shot", True)
    ye = swap(own, "shot", False)
    begun = early(corners, start_pressure, observed)
    passed = onward(x, c)
    yo2 = swap(passed, "shot", True)
    ye2 = swap(passed, "shot", False)
    cyo = swap(yo, "line", False)
    cye = swap(ye, "line", False)
    ce, co, cm, xe, xo, xm, oe, oo, om = wave(begun, own, ye, yo, c, x, ye2, yo2, cye, cyo)
    xo = swap(xo, "shot", True)
    xe = swap(xe, "shot", False)
    ce, co, cm = (swap(block, "line", False) for block in (ce, co, cm))
    oo = swap(merge(co, oo), "shot", True)
    xm, oe = combine(xm, xe, xo, ce, oe)
    xm = swap(xm, "line", True)
    oe = swap(oe, "shot", False)
    return total(om, cm, xm, oe, oo)


def solution(mesh):
    placed = (P("line", "shot", None),) * 5
    return jax.shard_map(
        body,
        mesh=mesh,
        in_specs=placed,
        out_specs=(P("line", "shot", None),) * 2,
        check_vma=False,
    )
```

```python
import jax
import jax.numpy as jnp
from jax import lax
from jax.experimental import pallas as pl
from jax.experimental.pallas import tpu as pltpu
from jax.sharding import PartitionSpec as P

coeffs = (1225.0 / 1024.0, -245.0 / 3072.0, 49.0 / 5120.0, -5.0 / 7168.0)
UNIT = coeffs[0] / 105.0
wavelet = (20.0, -12.0)

BLOCK = 16
APER = 32
NZ = 128
ROWS = 8
EXTRA = 1
F32 = jnp.float32
small = pltpu.CompilerParams(vmem_limit_bytes=4 << 20)


def swap_pairs(odd):
    pairs = []
    for i in range(1 if odd else 0, 15, 2):
        pairs += [(i, i + 1), (i + 1, i)]
    return pairs


def swap(block, axis, odd):
    return lax.ppermute(block, axis, swap_pairs(odd))


def vmem(count):
    return [pl.BlockSpec(memory_space=pltpu.VMEM)] * count


def offset_in_frame(corner_ref, dim, axis):
    return corner_ref[dim, 0] - (lax.axis_index(axis) - 1) * BLOCK


def side(axis, odd):
    even = lax.rem(lax.axis_index(axis), 2) == 0
    return pl.multiple_of(jnp.where(even, 0, 2 * BLOCK) if odd else jnp.where(even, 2 * BLOCK, 0), BLOCK)


def stencil(window):
    rows = window.shape[0] - 7
    total = None
    for m in range(1, 5):
        part = coeffs[m - 1] * (window[3 + m : 3 + m + rows] - window[4 - m : 4 - m + rows])
        total = part if total is None else total + part
    return total


def band(size, run, first, source_dim):
    source = lax.broadcasted_iota(jnp.int32, (size, size), source_dim)
    target = lax.broadcasted_iota(jnp.int32, (size, size), 1 - source_dim)
    away = source - target + first
    total = jnp.zeros((size, size), F32)
    for m in range(1, 5):
        value = coeffs[m - 1] / UNIT
        total = jnp.where(away == m, value, total)
        total = jnp.where(away == 1 - m, -value, total)
    return jnp.where(source // run == target // run, total, 0.0)


def halves(values):
    flat = values.reshape(-1, NZ)
    upper = flat.astype(jnp.bfloat16)
    lower = (flat - upper.astype(F32)).astype(jnp.bfloat16)
    return jnp.concatenate([upper, lower], axis=1)


def along_depth(both, matrix):
    return jnp.dot(both, matrix, preferred_element_type=F32).reshape(ROWS, APER, NZ)


def along_width(both, matrix):
    out = jnp.dot(matrix, both, preferred_element_type=F32)
    return (out[:, :NZ] + out[:, NZ:]).reshape(ROWS, APER, NZ)


def chunks():
    return range(0, APER, ROWS)


def plus_all(field, i0, wide, deep):
    both = halves(field[4 + i0 : 4 + i0 + ROWS])
    return (
        stencil(field[1 + i0 : 8 + i0 + ROWS]),
        along_width(both, wide),
        along_depth(both, deep),
    )


def early_kernel(corner_ref, p0_ref, obs_ref, field, g1, wide, deep, obs_out, corner_out):
    obs_out[...] = obs_ref[...]
    row = lax.broadcasted_iota(jnp.int32, (8, NZ), 0)
    corner_out[...] = jnp.where(row == 0, corner_ref[0, 0, 0], corner_ref[0, 0, 1])
    for first in range(2):
        wide[first] = band(ROWS * APER, APER, first, 1).astype(jnp.bfloat16)
        half = band(NZ, NZ, first, 0).astype(jnp.bfloat16)
        deep[first] = jnp.concatenate([half, half], axis=0)
    field[0:4] = jnp.zeros((4, APER, NZ), F32)
    field[36:40] = jnp.zeros((4, APER, NZ), F32)
    field[4:36] = p0_ref[...]
    for i0 in chunks():
        for k, g in enumerate(plus_all(field, i0, wide[0], deep[0])):
            g1[k, i0 : i0 + ROWS] = g


def early(corners, p0, obs):
    return pl.pallas_call(
        early_kernel,
        out_shape=(
            jax.ShapeDtypeStruct((APER + 8, APER, NZ), F32),
            jax.ShapeDtypeStruct((3, APER, APER, NZ), F32),
            jax.ShapeDtypeStruct((2, ROWS * APER, ROWS * APER), jnp.bfloat16),
            jax.ShapeDtypeStruct((2, 2 * NZ, NZ), jnp.bfloat16),
            jax.ShapeDtypeStruct((APER, APER, NZ), F32),
            jax.ShapeDtypeStruct((8, NZ), jnp.int32),
        ),
        in_specs=[pl.BlockSpec(memory_space=pltpu.SMEM)] + vmem(2),
        out_specs=tuple(vmem(6)),
        compiler_params=pltpu.CompilerParams(vmem_limit_bytes=8 << 20),
        name="early",
    )(corners, p0, obs)


def wave_kernel(
    field0, g1, wide, deep, obs_ref, corner_vmem, own_ref, yo_ref, ye_ref, c_ref, x_ref, ye2_ref, yo2_ref, cye_ref, cyo_ref,
    ce_out, co_out, cm_out, xe_out, xo_out, xm_out, oe_out, oo_out, om_out,
    corner_ref, sem, model, terms, field, bx, by, bz, gs, a1, a2, lam, kap, buoy, quad,
):
    corner_copy = pltpu.make_async_copy(corner_vmem, corner_ref, sem)
    corner_copy.start()
    row_c, row_x = side("line", False), side("line", True)
    col_e, col_o = side("shot", False), side("shot", True)
    middle = slice(BLOCK, 2 * BLOCK)

    for f in range(2):
        rows = slice(f * BLOCK, (f + 1) * BLOCK)
        model[f, middle, middle] = own_ref[rows]
        model[f, middle, pl.ds(col_e, BLOCK)] = ye_ref[rows]
        model[f, middle, pl.ds(col_o, BLOCK)] = yo_ref[rows]
        model[f, pl.ds(row_c, BLOCK), middle] = c_ref[rows]
        model[f, pl.ds(row_c, BLOCK), pl.ds(col_e, BLOCK)] = cye_ref[rows]
        model[f, pl.ds(row_c, BLOCK), pl.ds(col_o, BLOCK)] = cyo_ref[rows]
        model[f, pl.ds(row_x, BLOCK), middle] = x_ref[rows]
        model[f, pl.ds(row_x, BLOCK), pl.ds(col_e, BLOCK)] = ye2_ref[rows]
        model[f, pl.ds(row_x, BLOCK), pl.ds(col_o, BLOCK)] = yo2_ref[rows]
        terms[f] = jnp.zeros((48, 48, NZ), F32)

    for padded in (field, bx):
        padded[0:4] = jnp.zeros((4, APER, NZ), F32)
        padded[36:40] = jnp.zeros((4, APER, NZ), F32)

    corner_copy.wait()
    ox = offset_in_frame(corner_ref, 0, "line")
    oy = offset_in_frame(corner_ref, 1, "shot")

    def scaled(i0, values):
        rows = slice(i0, i0 + ROWS)
        light = buoy[rows]
        bx[4 + i0 : 4 + i0 + ROWS] = light * values[0]
        light = light * (UNIT * UNIT)
        by[rows] = light * values[1]
        bz[rows] = light * values[2]

    def minus(i0):
        rows = slice(i0, i0 + ROWS)
        spread = along_width(halves(by[rows]), wide[1]) + along_depth(halves(bz[rows]), deep[1])
        return spread + stencil(bx[i0 : i0 + ROWS + 7])

    def dotted(h, g):
        return h[0] * g[0] + (UNIT * UNIT) * (h[1] * g[1] + h[2] * g[2])

    row = lax.broadcasted_iota(jnp.int32, (8, NZ), 0)
    lane = lax.broadcasted_iota(jnp.int32, (8, NZ), 1)
    centre = jnp.where((row == 0) & (lane == 64), 1.0, 0.0)

    for i0 in chunks():
        rows = slice(i0, i0 + ROWS)
        for i in range(i0, i0 + ROWS):
            slot = ox + i
            speed = model[0, slot, pl.ds(oy, APER)]
            dense = model[1, slot, pl.ds(oy, APER)]
            kap[i] = 0.1 * dense * speed * speed
            buoy[i] = 0.1 / dense
        scaled(i0, [g1[k, rows] for k in range(3)])

    for i0 in chunks():
        rows = slice(i0, i0 + ROWS)
        inner = slice(4 + i0, 4 + i0 + ROWS)
        spread = minus(i0)
        a1[rows] = spread
        field[inner] = field0[inner] + kap[rows] * spread
    field[20, 16:24] += wavelet[0] * centre

    for i0 in chunks():
        rows = slice(i0, i0 + ROWS)
        g = plus_all(field, i0, wide[0], deep[0])
        both = [g1[k, rows] + g[k] for k in range(3)]
        for k in range(3):
            gs[k, rows] = both[k]
        scaled(i0, both)
    field[20, 16:24] += wavelet[1] * centre

    for i0 in chunks():
        rows = slice(i0, i0 + ROWS)
        inner = slice(4 + i0, 4 + i0 + ROWS)
        spread = minus(i0)
        a2[rows] = spread
        stiff = kap[rows]
        value = field[inner] + stiff * spread - obs_ref[rows]
        lam[rows] = value
        field[inner] = stiff * value

    for i0 in chunks():
        rows = slice(i0, i0 + ROWS)
        h = plus_all(field, i0, wide[0], deep[0])
        quad[rows] = dotted(h, [gs[k, rows] for k in range(3)])
        scaled(i0, h)

    for i0 in chunks():
        rows = slice(i0, i0 + ROWS)
        inner = slice(4 + i0, 4 + i0 + ROWS)
        late = lam[rows]
        early = late + minus(i0)
        field[inner] = kap[rows] * early
        lam[rows] = late * a2[rows] + early * a1[rows]

    for i0 in chunks():
        rows = slice(i0, i0 + ROWS)
        h = plus_all(field, i0, wide[0], deep[0])
        quad[rows] += dotted(h, [g1[k, rows] for k in range(3)])
        for i in range(i0, i0 + ROWS):
            slot = ox + i
            speed = model[0, slot, pl.ds(oy, APER)]
            dense = model[1, slot, pl.ds(oy, APER)]
            light = buoy[i]
            stiff = lam[i]
            terms[0, slot, pl.ds(oy, APER)] = 0.2 * dense * speed * stiff
            terms[1, slot, pl.ds(oy, APER)] = 0.1 * speed * speed * stiff + 10.0 * light * light * quad[i]

    for f in range(2):
        rows = slice(f * BLOCK, (f + 1) * BLOCK)
        ce_out[rows] = terms[f, pl.ds(row_c, BLOCK), pl.ds(col_e, BLOCK)]
        co_out[rows] = terms[f, pl.ds(row_c, BLOCK), pl.ds(col_o, BLOCK)]
        cm_out[rows] = terms[f, pl.ds(row_c, BLOCK), middle]
        xe_out[rows] = terms[f, pl.ds(row_x, BLOCK), pl.ds(col_e, BLOCK)]
        xo_out[rows] = terms[f, pl.ds(row_x, BLOCK), pl.ds(col_o, BLOCK)]
        xm_out[rows] = terms[f, pl.ds(row_x, BLOCK), middle]
        oe_out[rows] = terms[f, middle, pl.ds(col_e, BLOCK)]
        oo_out[rows] = terms[f, middle, pl.ds(col_o, BLOCK)]
        om_out[rows] = terms[f, middle, middle]
    for out_ref in (xe_out, xo_out):
        out_ref[2 * BLOCK :] = jnp.zeros((2 * EXTRA, BLOCK, NZ), F32)


part = jax.ShapeDtypeStruct((2 * BLOCK, BLOCK, NZ), F32)
early_part = jax.ShapeDtypeStruct((2 * BLOCK + 2 * EXTRA, BLOCK, NZ), F32)


def wave(begun, *blocks):
    cube = pltpu.VMEM((APER, APER, NZ), F32)
    padded = pltpu.VMEM((APER + 8, APER, NZ), F32)
    return pl.pallas_call(
        wave_kernel,
        out_shape=(part,) * 3 + (early_part,) * 2 + (part,) * 4,
        in_specs=vmem(15),
        out_specs=tuple(vmem(9)),
        scratch_shapes=[
            pltpu.SMEM((8, NZ), jnp.int32),
            pltpu.SemaphoreType.DMA,
            pltpu.VMEM((2, 48, 48, NZ), F32),
            pltpu.VMEM((2, 48, 48, NZ), F32),
            padded, padded, cube, cube,
            pltpu.VMEM((3, APER, APER, NZ), F32),
            cube, cube, cube, cube, cube, cube,
        ],
        compiler_params=pltpu.CompilerParams(vmem_limit_bytes=26 << 20),
        name="wave",
    )(*begun, *blocks)


def onward_kernel(x_ref, c_ref, out_ref):
    del c_ref
    out_ref[...] = x_ref[...]


def onward(x, c):
    return pl.pallas_call(
        onward_kernel,
        out_shape=part,
        in_specs=vmem(1) + [pl.BlockSpec(memory_space=pl.ANY)],
        out_specs=vmem(1)[0],
        compiler_params=small,
        name="onward",
    )(x, c)


def merge_kernel(c_ref, o_ref, out_ref):
    out_ref[: 2 * BLOCK] = o_ref[...] + c_ref[...]
    out_ref[2 * BLOCK :] = jnp.zeros((EXTRA, BLOCK, NZ), F32)


def merge(c, o):
    return pl.pallas_call(
        merge_kernel,
        out_shape=jax.ShapeDtypeStruct((2 * BLOCK + EXTRA, BLOCK, NZ), F32),
        in_specs=vmem(2),
        out_specs=vmem(1)[0],
        compiler_params=small,
        name="merge",
    )(c, o)


def combine_kernel(m_ref, o_ref, e_ref, c_ref, oe_ref, out_ref, oe_out):
    out_ref[...] = m_ref[...] + e_ref[: 2 * BLOCK] + o_ref[: 2 * BLOCK]
    oe_out[...] = oe_ref[...] + c_ref[...]


def combine(m, e, o, c, oe):
    return pl.pallas_call(
        combine_kernel,
        out_shape=(part, part),
        in_specs=vmem(5),
        out_specs=tuple(vmem(2)),
        compiler_params=small,
        name="combine",
    )(m, o, e, c, oe)


def total_kernel(own_ref, c_ref, x_ref, e_ref, o_ref, vel_ref, rho_ref):
    for f, out_ref in ((0, vel_ref), (1, rho_ref)):
        rows = slice(f * BLOCK, (f + 1) * BLOCK)
        out_ref[...] = ((own_ref[rows] + c_ref[rows]) + x_ref[rows]) + (e_ref[rows] + o_ref[rows])


def total(*parts):
    block = jax.ShapeDtypeStruct((BLOCK, BLOCK, NZ), F32)
    return pl.pallas_call(
        total_kernel,
        out_shape=(block, block),
        in_specs=vmem(5),
        out_specs=tuple(vmem(2)),
        compiler_params=small,
        name="total",
    )(*parts)


def body(velocity, density, start_pressure, observed, corners):
    own = jnp.stack([velocity, density]).reshape(2 * BLOCK, BLOCK, NZ)
    c = swap(own, "line", False)
    x = swap(own, "line", True)
    yo = swap(own, "shot", True)
    ye = swap(own, "shot", False)
    begun = early(corners, start_pressure, observed)
    passed = onward(x, c)
    yo2 = swap(passed, "shot", True)
    ye2 = swap(passed, "shot", False)
    cyo = swap(yo, "line", False)
    cye = swap(ye, "line", False)
    ce, co, cm, xe, xo, xm, oe, oo, om = wave(begun, own, yo, ye, c, x, ye2, yo2, cye, cyo)
    xo = swap(xo, "shot", True)
    xe = swap(xe, "shot", False)
    ce, co, cm = (swap(block, "line", False) for block in (ce, co, cm))
    oo = swap(merge(co, oo), "shot", True)
    xm, oe = combine(xm, xe, xo, ce, oe)
    xm = swap(xm, "line", True)
    oe = swap(oe, "shot", False)
    return total(om, cm, xm, oe, oo)


def solution(mesh):
    placed = (P("line", "shot", None),) * 5
    return jax.shard_map(
        body,
        mesh=mesh,
        in_specs=placed,
        out_specs=(P("line", "shot", None),) * 2,
        check_vma=False,
    )
```

```python
import jax
import jax.numpy as jnp
from jax import lax
from jax.experimental import pallas as pl
from jax.experimental.pallas import tpu as pltpu
from jax.sharding import PartitionSpec as P

coeffs = (1225.0 / 1024.0, -245.0 / 3072.0, 49.0 / 5120.0, -5.0 / 7168.0)
UNIT = coeffs[0] / 105.0
wavelet = (20.0, -12.0)

BLOCK = 16
APER = 32
NZ = 128
ROWS = 8
EXTRA = 1
F32 = jnp.float32
small = pltpu.CompilerParams(vmem_limit_bytes=4 << 20)


def swap_pairs(odd):
    pairs = []
    for i in range(1 if odd else 0, 15, 2):
        pairs += [(i, i + 1), (i + 1, i)]
    return pairs


def swap(block, axis, odd):
    return lax.ppermute(block, axis, swap_pairs(odd))


def vmem(count):
    return [pl.BlockSpec(memory_space=pltpu.VMEM)] * count


def offset_in_frame(corner_ref, dim, axis):
    return corner_ref[dim, 0] - (lax.axis_index(axis) - 1) * BLOCK


def side(axis, odd):
    even = lax.rem(lax.axis_index(axis), 2) == 0
    return pl.multiple_of(jnp.where(even, 0, 2 * BLOCK) if odd else jnp.where(even, 2 * BLOCK, 0), BLOCK)


def stencil(window):
    rows = window.shape[0] - 7
    total = None
    for m in range(1, 5):
        part = coeffs[m - 1] * (window[3 + m : 3 + m + rows] - window[4 - m : 4 - m + rows])
        total = part if total is None else total + part
    return total


def band(size, run, first, source_dim):
    source = lax.broadcasted_iota(jnp.int32, (size, size), source_dim)
    target = lax.broadcasted_iota(jnp.int32, (size, size), 1 - source_dim)
    away = source - target + first
    total = jnp.zeros((size, size), F32)
    for m in range(1, 5):
        value = coeffs[m - 1] / UNIT
        total = jnp.where(away == m, value, total)
        total = jnp.where(away == 1 - m, -value, total)
    return jnp.where(source // run == target // run, total, 0.0)


def halves(values):
    flat = values.reshape(-1, NZ)
    upper = flat.astype(jnp.bfloat16)
    lower = (flat - upper.astype(F32)).astype(jnp.bfloat16)
    return jnp.concatenate([upper, lower], axis=1)


def along_depth(both, matrix):
    return jnp.dot(both, matrix, preferred_element_type=F32).reshape(ROWS, APER, NZ)


def along_width(both, matrix):
    out = jnp.dot(matrix, both, preferred_element_type=F32)
    return (out[:, :NZ] + out[:, NZ:]).reshape(ROWS, APER, NZ)


def chunks():
    return range(0, APER, ROWS)


def plus_all(field, i0, wide, deep):
    both = halves(field[4 + i0 : 4 + i0 + ROWS])
    return (
        stencil(field[1 + i0 : 8 + i0 + ROWS]),
        along_width(both, wide),
        along_depth(both, deep),
    )


def early_kernel(corner_ref, p0_ref, obs_ref, field, g1, wide, deep, obs_out, corner_out):
    obs_out[...] = obs_ref[...]
    row = lax.broadcasted_iota(jnp.int32, (8, NZ), 0)
    corner_out[...] = jnp.where(row == 0, corner_ref[0, 0, 0], corner_ref[0, 0, 1])
    for first in range(2):
        wide[first] = band(ROWS * APER, APER, first, 1).astype(jnp.bfloat16)
        half = band(NZ, NZ, first, 0).astype(jnp.bfloat16)
        deep[first] = jnp.concatenate([half, half], axis=0)
    field[0:4] = jnp.zeros((4, APER, NZ), F32)
    field[36:40] = jnp.zeros((4, APER, NZ), F32)
    field[4:36] = p0_ref[...]
    for i0 in chunks():
        for k, g in enumerate(plus_all(field, i0, wide[0], deep[0])):
            g1[k, i0 : i0 + ROWS] = g


def early(corners, p0, obs):
    return pl.pallas_call(
        early_kernel,
        out_shape=(
            jax.ShapeDtypeStruct((APER + 8, APER, NZ), F32),
            jax.ShapeDtypeStruct((3, APER, APER, NZ), F32),
            jax.ShapeDtypeStruct((2, ROWS * APER, ROWS * APER), jnp.bfloat16),
            jax.ShapeDtypeStruct((2, 2 * NZ, NZ), jnp.bfloat16),
            jax.ShapeDtypeStruct((APER, APER, NZ), F32),
            jax.ShapeDtypeStruct((8, NZ), jnp.int32),
        ),
        in_specs=[pl.BlockSpec(memory_space=pltpu.SMEM)] + vmem(2),
        out_specs=tuple(vmem(6)),
        compiler_params=pltpu.CompilerParams(vmem_limit_bytes=8 << 20),
        name="early",
    )(corners, p0, obs)


def wave_kernel(
    field0, g1, wide, deep, obs_ref, corner_vmem, own_ref, yo_ref, ye_ref, c_ref, x_ref, ye2_ref, yo2_ref, cye_ref, cyo_ref,
    ce_out, co_out, cm_out, xe_out, xo_out, xm_out, oe_out, oo_out, om_out,
    corner_ref, sem, model, terms, field, bx, by, bz, gs, a1, a2, lam, kap, buoy, quad,
):
    corner_copy = pltpu.make_async_copy(corner_vmem, corner_ref, sem)
    corner_copy.start()
    row_c, row_x = side("line", False), side("line", True)
    col_e, col_o = side("shot", False), side("shot", True)
    middle = slice(BLOCK, 2 * BLOCK)

    for f in range(2):
        rows = slice(f * BLOCK, (f + 1) * BLOCK)
        model[f, middle, middle] = own_ref[rows]
        model[f, middle, pl.ds(col_e, BLOCK)] = ye_ref[rows]
        model[f, middle, pl.ds(col_o, BLOCK)] = yo_ref[rows]
        model[f, pl.ds(row_c, BLOCK), middle] = c_ref[rows]
        model[f, pl.ds(row_c, BLOCK), pl.ds(col_e, BLOCK)] = cye_ref[rows]
        model[f, pl.ds(row_c, BLOCK), pl.ds(col_o, BLOCK)] = cyo_ref[rows]
        model[f, pl.ds(row_x, BLOCK), middle] = x_ref[rows]
        model[f, pl.ds(row_x, BLOCK), pl.ds(col_e, BLOCK)] = ye2_ref[rows]
        model[f, pl.ds(row_x, BLOCK), pl.ds(col_o, BLOCK)] = yo2_ref[rows]
        terms[f] = jnp.zeros((48, 48, NZ), F32)

    for padded in (field, bx):
        padded[0:4] = jnp.zeros((4, APER, NZ), F32)
        padded[36:40] = jnp.zeros((4, APER, NZ), F32)

    corner_copy.wait()
    ox = offset_in_frame(corner_ref, 0, "line")
    oy = offset_in_frame(corner_ref, 1, "shot")

    def scaled(i0, values):
        rows = slice(i0, i0 + ROWS)
        light = buoy[rows]
        bx[4 + i0 : 4 + i0 + ROWS] = light * values[0]
        light = light * (UNIT * UNIT)
        by[rows] = light * values[1]
        bz[rows] = light * values[2]

    def minus(i0):
        rows = slice(i0, i0 + ROWS)
        spread = along_width(halves(by[rows]), wide[1]) + along_depth(halves(bz[rows]), deep[1])
        return spread + stencil(bx[i0 : i0 + ROWS + 7])

    def dotted(h, g):
        return h[0] * g[0] + (UNIT * UNIT) * (h[1] * g[1] + h[2] * g[2])

    row = lax.broadcasted_iota(jnp.int32, (8, NZ), 0)
    lane = lax.broadcasted_iota(jnp.int32, (8, NZ), 1)
    centre = jnp.where((row == 0) & (lane == 64), 1.0, 0.0)

    for i0 in chunks():
        rows = slice(i0, i0 + ROWS)
        for i in range(i0, i0 + ROWS):
            slot = ox + i
            speed = model[0, slot, pl.ds(oy, APER)]
            dense = model[1, slot, pl.ds(oy, APER)]
            kap[i] = 0.1 * dense * speed * speed
            buoy[i] = 0.1 / dense
        scaled(i0, [g1[k, rows] for k in range(3)])

    for i0 in chunks():
        rows = slice(i0, i0 + ROWS)
        inner = slice(4 + i0, 4 + i0 + ROWS)
        spread = minus(i0)
        a1[rows] = spread
        field[inner] = field0[inner] + kap[rows] * spread
    field[20, 16:24] += wavelet[0] * centre

    for i0 in chunks():
        rows = slice(i0, i0 + ROWS)
        g = plus_all(field, i0, wide[0], deep[0])
        both = [g1[k, rows] + g[k] for k in range(3)]
        for k in range(3):
            gs[k, rows] = both[k]
        scaled(i0, both)
    field[20, 16:24] += wavelet[1] * centre

    for i0 in chunks():
        rows = slice(i0, i0 + ROWS)
        inner = slice(4 + i0, 4 + i0 + ROWS)
        spread = minus(i0)
        a2[rows] = spread
        stiff = kap[rows]
        value = field[inner] + stiff * spread - obs_ref[rows]
        lam[rows] = value
        field[inner] = stiff * value

    for i0 in chunks():
        rows = slice(i0, i0 + ROWS)
        h = plus_all(field, i0, wide[0], deep[0])
        quad[rows] = dotted(h, [gs[k, rows] for k in range(3)])
        scaled(i0, h)

    for i0 in chunks():
        rows = slice(i0, i0 + ROWS)
        inner = slice(4 + i0, 4 + i0 + ROWS)
        late = lam[rows]
        early = late + minus(i0)
        field[inner] = kap[rows] * early
        lam[rows] = late * a2[rows] + early * a1[rows]

    for i0 in chunks():
        rows = slice(i0, i0 + ROWS)
        h = plus_all(field, i0, wide[0], deep[0])
        quad[rows] += dotted(h, [g1[k, rows] for k in range(3)])
        for i in range(i0, i0 + ROWS):
            slot = ox + i
            speed = model[0, slot, pl.ds(oy, APER)]
            dense = model[1, slot, pl.ds(oy, APER)]
            light = buoy[i]
            stiff = lam[i]
            terms[0, slot, pl.ds(oy, APER)] = 0.2 * dense * speed * stiff
            terms[1, slot, pl.ds(oy, APER)] = 0.1 * speed * speed * stiff + 10.0 * light * light * quad[i]

    for f in range(2):
        rows = slice(f * BLOCK, (f + 1) * BLOCK)
        ce_out[rows] = terms[f, pl.ds(row_c, BLOCK), pl.ds(col_e, BLOCK)]
        co_out[rows] = terms[f, pl.ds(row_c, BLOCK), pl.ds(col_o, BLOCK)]
        cm_out[rows] = terms[f, pl.ds(row_c, BLOCK), middle]
        xe_out[rows] = terms[f, pl.ds(row_x, BLOCK), pl.ds(col_e, BLOCK)]
        xo_out[rows] = terms[f, pl.ds(row_x, BLOCK), pl.ds(col_o, BLOCK)]
        xm_out[rows] = terms[f, pl.ds(row_x, BLOCK), middle]
        oe_out[rows] = terms[f, middle, pl.ds(col_e, BLOCK)]
        oo_out[rows] = terms[f, middle, pl.ds(col_o, BLOCK)]
        om_out[rows] = terms[f, middle, middle]
    for out_ref in (xe_out, xo_out):
        out_ref[2 * BLOCK :] = jnp.zeros((2 * EXTRA, BLOCK, NZ), F32)


part = jax.ShapeDtypeStruct((2 * BLOCK, BLOCK, NZ), F32)
early_part = jax.ShapeDtypeStruct((2 * BLOCK + 2 * EXTRA, BLOCK, NZ), F32)


def wave(begun, *blocks):
    cube = pltpu.VMEM((APER, APER, NZ), F32)
    padded = pltpu.VMEM((APER + 8, APER, NZ), F32)
    return pl.pallas_call(
        wave_kernel,
        out_shape=(part,) * 3 + (early_part,) * 2 + (part,) * 4,
        in_specs=vmem(15),
        out_specs=tuple(vmem(9)),
        scratch_shapes=[
            pltpu.SMEM((8, NZ), jnp.int32),
            pltpu.SemaphoreType.DMA,
            pltpu.VMEM((2, 48, 48, NZ), F32),
            pltpu.VMEM((2, 48, 48, NZ), F32),
            padded, padded, cube, cube,
            pltpu.VMEM((3, APER, APER, NZ), F32),
            cube, cube, cube, cube, cube, cube,
        ],
        compiler_params=pltpu.CompilerParams(vmem_limit_bytes=26 << 20),
        name="wave",
    )(*begun, *blocks)


def onward_kernel(x_ref, c_ref, out_ref):
    del c_ref
    out_ref[...] = x_ref[...]


def onward(x, c):
    return pl.pallas_call(
        onward_kernel,
        out_shape=part,
        in_specs=vmem(1) + [pl.BlockSpec(memory_space=pl.ANY)],
        out_specs=vmem(1)[0],
        compiler_params=small,
        name="onward",
    )(x, c)


def merge_kernel(c_ref, o_ref, out_ref):
    out_ref[: 2 * BLOCK] = o_ref[...] + c_ref[...]
    out_ref[2 * BLOCK :] = jnp.zeros((EXTRA, BLOCK, NZ), F32)


def merge(c, o):
    return pl.pallas_call(
        merge_kernel,
        out_shape=jax.ShapeDtypeStruct((2 * BLOCK + EXTRA, BLOCK, NZ), F32),
        in_specs=vmem(2),
        out_specs=vmem(1)[0],
        compiler_params=small,
        name="merge",
    )(c, o)


def combine_kernel(m_ref, o_ref, e_ref, c_ref, oe_ref, out_ref, oe_out):
    out_ref[...] = m_ref[...] + e_ref[: 2 * BLOCK] + o_ref[: 2 * BLOCK]
    oe_out[...] = oe_ref[...] + c_ref[...]


def combine(m, e, o, c, oe):
    return pl.pallas_call(
        combine_kernel,
        out_shape=(part, part),
        in_specs=vmem(5),
        out_specs=tuple(vmem(2)),
        compiler_params=small,
        name="combine",
    )(m, o, e, c, oe)


def total_kernel(own_ref, c_ref, x_ref, e_ref, o_ref, vel_hbm, rho_hbm, held, sems):
    copies = []
    for f, out_hbm in ((0, vel_hbm), (1, rho_hbm)):
        rows = slice(f * BLOCK, (f + 1) * BLOCK)
        held[f] = ((own_ref[rows] + c_ref[rows]) + x_ref[rows]) + (e_ref[rows] + o_ref[rows])
        copies.append(pltpu.make_async_copy(held.at[f], out_hbm, sems.at[f]))
        copies[f].start()
    for copy in copies:
        copy.wait()


def total(*parts):
    block = jax.ShapeDtypeStruct((BLOCK, BLOCK, NZ), F32)
    return pl.pallas_call(
        total_kernel,
        out_shape=(block, block),
        in_specs=vmem(5),
        out_specs=(pl.BlockSpec(memory_space=pltpu.HBM),) * 2,
        scratch_shapes=[pltpu.VMEM((2, BLOCK, BLOCK, NZ), F32), pltpu.SemaphoreType.DMA((2,))],
        compiler_params=small,
        name="total",
    )(*parts)


def body(velocity, density, start_pressure, observed, corners):
    own = jnp.stack([velocity, density]).reshape(2 * BLOCK, BLOCK, NZ)
    c = swap(own, "line", False)
    x = swap(own, "line", True)
    yo = swap(own, "shot", True)
    ye = swap(own, "shot", False)
    begun = early(corners, start_pressure, observed)
    passed = onward(x, c)
    yo2 = swap(passed, "shot", True)
    ye2 = swap(passed, "shot", False)
    cyo = swap(yo, "line", False)
    cye = swap(ye, "line", False)
    ce, co, cm, xe, xo, xm, oe, oo, om = wave(begun, own, yo, ye, c, x, ye2, yo2, cye, cyo)
    xo = swap(xo, "shot", True)
    xe = swap(xe, "shot", False)
    ce, co, cm = (swap(block, "line", False) for block in (ce, co, cm))
    oo = swap(merge(co, oo), "shot", True)
    xm, oe = combine(xm, xe, xo, ce, oe)
    xm = swap(xm, "line", True)
    oe = swap(oe, "shot", False)
    return total(om, cm, xm, oe, oo)


def solution(mesh):
    placed = (P("line", "shot", None),) * 5
    return jax.shard_map(
        body,
        mesh=mesh,
        in_specs=placed,
        out_specs=(P("line", "shot", None),) * 2,
        check_vma=False,
    )
```

```python
import jax
import jax.numpy as jnp
from jax import lax
from jax.experimental import pallas as pl
from jax.experimental.pallas import tpu as pltpu
from jax.sharding import PartitionSpec as P

coeffs = (1225.0 / 1024.0, -245.0 / 3072.0, 49.0 / 5120.0, -5.0 / 7168.0)
UNIT = coeffs[0] / 105.0
wavelet = (20.0, -12.0)

BLOCK = 16
APER = 32
NZ = 128
ROWS = 4
EXTRA = 1
F32 = jnp.float32
small = pltpu.CompilerParams(vmem_limit_bytes=4 << 20)


def swap_pairs(odd):
    pairs = []
    for i in range(1 if odd else 0, 15, 2):
        pairs += [(i, i + 1), (i + 1, i)]
    return pairs


def swap(block, axis, odd):
    return lax.ppermute(block, axis, swap_pairs(odd))


def vmem(count):
    return [pl.BlockSpec(memory_space=pltpu.VMEM)] * count


def offset_in_frame(corner_ref, dim, axis):
    return corner_ref[dim, 0] - (lax.axis_index(axis) - 1) * BLOCK


def side(axis, odd):
    even = lax.rem(lax.axis_index(axis), 2) == 0
    return pl.multiple_of(jnp.where(even, 0, 2 * BLOCK) if odd else jnp.where(even, 2 * BLOCK, 0), BLOCK)


def stencil(window):
    rows = window.shape[0] - 7
    total = None
    for m in range(1, 5):
        part = coeffs[m - 1] * (window[3 + m : 3 + m + rows] - window[4 - m : 4 - m + rows])
        total = part if total is None else total + part
    return total


def band(size, run, first, source_dim):
    source = lax.broadcasted_iota(jnp.int32, (size, size), source_dim)
    target = lax.broadcasted_iota(jnp.int32, (size, size), 1 - source_dim)
    away = source - target + first
    total = jnp.zeros((size, size), F32)
    for m in range(1, 5):
        value = coeffs[m - 1] / UNIT
        total = jnp.where(away == m, value, total)
        total = jnp.where(away == 1 - m, -value, total)
    return jnp.where(source // run == target // run, total, 0.0)


def halves(values):
    flat = values.reshape(-1, NZ)
    upper = flat.astype(jnp.bfloat16)
    lower = (flat - upper.astype(F32)).astype(jnp.bfloat16)
    return jnp.concatenate([upper, lower], axis=1)


def along_depth(both, matrix):
    return jnp.dot(both, matrix, preferred_element_type=F32).reshape(ROWS, APER, NZ)


def along_width(both, matrix):
    out = jnp.dot(matrix, both, preferred_element_type=F32)
    return (out[:, :NZ] + out[:, NZ:]).reshape(ROWS, APER, NZ)


def chunks():
    return range(0, APER, ROWS)


def plus_all(field, i0, wide, deep):
    both = halves(field[4 + i0 : 4 + i0 + ROWS])
    return (
        stencil(field[1 + i0 : 8 + i0 + ROWS]),
        along_width(both, wide),
        along_depth(both, deep),
    )


def early_kernel(corner_ref, p0_ref, obs_ref, field, g1, wide, deep, obs_out, corner_out):
    obs_out[...] = obs_ref[...]
    row = lax.broadcasted_iota(jnp.int32, (8, NZ), 0)
    corner_out[...] = jnp.where(row == 0, corner_ref[0, 0, 0], corner_ref[0, 0, 1])
    for first in range(2):
        wide[first] = band(ROWS * APER, APER, first, 1).astype(jnp.bfloat16)
        half = band(NZ, NZ, first, 0).astype(jnp.bfloat16)
        deep[first] = jnp.concatenate([half, half], axis=0)
    field[0:4] = jnp.zeros((4, APER, NZ), F32)
    field[36:40] = jnp.zeros((4, APER, NZ), F32)
    field[4:36] = p0_ref[...]
    for i0 in chunks():
        for k, g in enumerate(plus_all(field, i0, wide[0], deep[0])):
            g1[k, i0 : i0 + ROWS] = g


def early(corners, p0, obs):
    return pl.pallas_call(
        early_kernel,
        out_shape=(
            jax.ShapeDtypeStruct((APER + 8, APER, NZ), F32),
            jax.ShapeDtypeStruct((3, APER, APER, NZ), F32),
            jax.ShapeDtypeStruct((2, ROWS * APER, ROWS * APER), jnp.bfloat16),
            jax.ShapeDtypeStruct((2, 2 * NZ, NZ), jnp.bfloat16),
            jax.ShapeDtypeStruct((APER, APER, NZ), F32),
            jax.ShapeDtypeStruct((8, NZ), jnp.int32),
        ),
        in_specs=[pl.BlockSpec(memory_space=pltpu.SMEM)] + vmem(2),
        out_specs=tuple(vmem(6)),
        compiler_params=pltpu.CompilerParams(vmem_limit_bytes=8 << 20),
        name="early",
    )(corners, p0, obs)


def wave_kernel(
    field0, g1, wide, deep, obs_ref, corner_vmem, own_ref, yo_ref, ye_ref, c_ref, x_ref, ye2_ref, yo2_ref, cye_ref, cyo_ref,
    ce_out, co_out, cm_out, xe_out, xo_out, xm_out, oe_out, oo_out, om_out,
    corner_ref, sem, model, terms, field, bx, by, bz, gs, a1, a2, lam, kap, buoy, quad,
):
    corner_copy = pltpu.make_async_copy(corner_vmem, corner_ref, sem)
    corner_copy.start()
    row_c, row_x = side("line", False), side("line", True)
    col_e, col_o = side("shot", False), side("shot", True)
    middle = slice(BLOCK, 2 * BLOCK)

    for f in range(2):
        rows = slice(f * BLOCK, (f + 1) * BLOCK)
        model[f, middle, middle] = own_ref[rows]
        model[f, middle, pl.ds(col_e, BLOCK)] = ye_ref[rows]
        model[f, middle, pl.ds(col_o, BLOCK)] = yo_ref[rows]
        model[f, pl.ds(row_c, BLOCK), middle] = c_ref[rows]
        model[f, pl.ds(row_c, BLOCK), pl.ds(col_e, BLOCK)] = cye_ref[rows]
        model[f, pl.ds(row_c, BLOCK), pl.ds(col_o, BLOCK)] = cyo_ref[rows]
        model[f, pl.ds(row_x, BLOCK), middle] = x_ref[rows]
        model[f, pl.ds(row_x, BLOCK), pl.ds(col_e, BLOCK)] = ye2_ref[rows]
        model[f, pl.ds(row_x, BLOCK), pl.ds(col_o, BLOCK)] = yo2_ref[rows]
        terms[f] = jnp.zeros((48, 48, NZ), F32)

    for padded in (field, bx):
        padded[0:4] = jnp.zeros((4, APER, NZ), F32)
        padded[36:40] = jnp.zeros((4, APER, NZ), F32)

    corner_copy.wait()
    ox = offset_in_frame(corner_ref, 0, "line")
    oy = offset_in_frame(corner_ref, 1, "shot")

    def scaled(i0, values):
        rows = slice(i0, i0 + ROWS)
        light = buoy[rows]
        bx[4 + i0 : 4 + i0 + ROWS] = light * values[0]
        light = light * (UNIT * UNIT)
        by[rows] = light * values[1]
        bz[rows] = light * values[2]

    def minus(i0):
        rows = slice(i0, i0 + ROWS)
        spread = along_width(halves(by[rows]), wide[1]) + along_depth(halves(bz[rows]), deep[1])
        return spread + stencil(bx[i0 : i0 + ROWS + 7])

    def dotted(h, g):
        return h[0] * g[0] + (UNIT * UNIT) * (h[1] * g[1] + h[2] * g[2])

    row = lax.broadcasted_iota(jnp.int32, (8, NZ), 0)
    lane = lax.broadcasted_iota(jnp.int32, (8, NZ), 1)
    centre = jnp.where((row == 0) & (lane == 64), 1.0, 0.0)

    for i0 in chunks():
        rows = slice(i0, i0 + ROWS)
        for i in range(i0, i0 + ROWS):
            slot = ox + i
            speed = model[0, slot, pl.ds(oy, APER)]
            dense = model[1, slot, pl.ds(oy, APER)]
            kap[i] = 0.1 * dense * speed * speed
            buoy[i] = 0.1 / dense
        scaled(i0, [g1[k, rows] for k in range(3)])

    for i0 in chunks():
        rows = slice(i0, i0 + ROWS)
        inner = slice(4 + i0, 4 + i0 + ROWS)
        spread = minus(i0)
        a1[rows] = spread
        field[inner] = field0[inner] + kap[rows] * spread
    field[20, 16:24] += wavelet[0] * centre

    for i0 in chunks():
        rows = slice(i0, i0 + ROWS)
        g = plus_all(field, i0, wide[0], deep[0])
        both = [g1[k, rows] + g[k] for k in range(3)]
        for k in range(3):
            gs[k, rows] = both[k]
        scaled(i0, both)
    field[20, 16:24] += wavelet[1] * centre

    for i0 in chunks():
        rows = slice(i0, i0 + ROWS)
        inner = slice(4 + i0, 4 + i0 + ROWS)
        spread = minus(i0)
        a2[rows] = spread
        stiff = kap[rows]
        value = field[inner] + stiff * spread - obs_ref[rows]
        lam[rows] = value
        field[inner] = stiff * value

    for i0 in chunks():
        rows = slice(i0, i0 + ROWS)
        h = plus_all(field, i0, wide[0], deep[0])
        quad[rows] = dotted(h, [gs[k, rows] for k in range(3)])
        scaled(i0, h)

    for i0 in chunks():
        rows = slice(i0, i0 + ROWS)
        inner = slice(4 + i0, 4 + i0 + ROWS)
        late = lam[rows]
        early = late + minus(i0)
        field[inner] = kap[rows] * early
        lam[rows] = late * a2[rows] + early * a1[rows]

    for i0 in chunks():
        rows = slice(i0, i0 + ROWS)
        h = plus_all(field, i0, wide[0], deep[0])
        quad[rows] += dotted(h, [g1[k, rows] for k in range(3)])
        for i in range(i0, i0 + ROWS):
            slot = ox + i
            speed = model[0, slot, pl.ds(oy, APER)]
            dense = model[1, slot, pl.ds(oy, APER)]
            light = buoy[i]
            stiff = lam[i]
            terms[0, slot, pl.ds(oy, APER)] = 0.2 * dense * speed * stiff
            terms[1, slot, pl.ds(oy, APER)] = 0.1 * speed * speed * stiff + 10.0 * light * light * quad[i]

    for f in range(2):
        rows = slice(f * BLOCK, (f + 1) * BLOCK)
        ce_out[rows] = terms[f, pl.ds(row_c, BLOCK), pl.ds(col_e, BLOCK)]
        co_out[rows] = terms[f, pl.ds(row_c, BLOCK), pl.ds(col_o, BLOCK)]
        cm_out[rows] = terms[f, pl.ds(row_c, BLOCK), middle]
        xe_out[rows] = terms[f, pl.ds(row_x, BLOCK), pl.ds(col_e, BLOCK)]
        xo_out[rows] = terms[f, pl.ds(row_x, BLOCK), pl.ds(col_o, BLOCK)]
        xm_out[rows] = terms[f, pl.ds(row_x, BLOCK), middle]
        oe_out[rows] = terms[f, middle, pl.ds(col_e, BLOCK)]
        oo_out[rows] = terms[f, middle, pl.ds(col_o, BLOCK)]
        om_out[rows] = terms[f, middle, middle]
    for out_ref in (xe_out, xo_out):
        out_ref[2 * BLOCK :] = jnp.zeros((2 * EXTRA, BLOCK, NZ), F32)


part = jax.ShapeDtypeStruct((2 * BLOCK, BLOCK, NZ), F32)
early_part = jax.ShapeDtypeStruct((2 * BLOCK + 2 * EXTRA, BLOCK, NZ), F32)


def wave(begun, *blocks):
    cube = pltpu.VMEM((APER, APER, NZ), F32)
    padded = pltpu.VMEM((APER + 8, APER, NZ), F32)
    return pl.pallas_call(
        wave_kernel,
        out_shape=(part,) * 3 + (early_part,) * 2 + (part,) * 4,
        in_specs=vmem(15),
        out_specs=tuple(vmem(9)),
        scratch_shapes=[
            pltpu.SMEM((8, NZ), jnp.int32),
            pltpu.SemaphoreType.DMA,
            pltpu.VMEM((2, 48, 48, NZ), F32),
            pltpu.VMEM((2, 48, 48, NZ), F32),
            padded, padded, cube, cube,
            pltpu.VMEM((3, APER, APER, NZ), F32),
            cube, cube, cube, cube, cube, cube,
        ],
        compiler_params=pltpu.CompilerParams(vmem_limit_bytes=26 << 20),
        name="wave",
    )(*begun, *blocks)


def onward_kernel(x_ref, c_ref, out_ref):
    del c_ref
    out_ref[...] = x_ref[...]


def onward(x, c):
    return pl.pallas_call(
        onward_kernel,
        out_shape=part,
        in_specs=vmem(1) + [pl.BlockSpec(memory_space=pl.ANY)],
        out_specs=vmem(1)[0],
        compiler_params=small,
        name="onward",
    )(x, c)


def merge_kernel(c_ref, o_ref, out_ref):
    out_ref[: 2 * BLOCK] = o_ref[...] + c_ref[...]
    out_ref[2 * BLOCK :] = jnp.zeros((EXTRA, BLOCK, NZ), F32)


def merge(c, o):
    return pl.pallas_call(
        merge_kernel,
        out_shape=jax.ShapeDtypeStruct((2 * BLOCK + EXTRA, BLOCK, NZ), F32),
        in_specs=vmem(2),
        out_specs=vmem(1)[0],
        compiler_params=small,
        name="merge",
    )(c, o)


def combine_kernel(m_ref, o_ref, e_ref, c_ref, oe_ref, out_ref, oe_out):
    out_ref[...] = m_ref[...] + e_ref[: 2 * BLOCK] + o_ref[: 2 * BLOCK]
    oe_out[...] = oe_ref[...] + c_ref[...]


def combine(m, e, o, c, oe):
    return pl.pallas_call(
        combine_kernel,
        out_shape=(part, part),
        in_specs=vmem(5),
        out_specs=tuple(vmem(2)),
        compiler_params=small,
        name="combine",
    )(m, o, e, c, oe)


def total_kernel(own_ref, c_ref, x_ref, e_ref, o_ref, vel_hbm, rho_hbm, held, sems):
    copies = []
    for f, out_hbm in ((0, vel_hbm), (1, rho_hbm)):
        rows = slice(f * BLOCK, (f + 1) * BLOCK)
        held[f] = ((own_ref[rows] + c_ref[rows]) + x_ref[rows]) + (e_ref[rows] + o_ref[rows])
        copies.append(pltpu.make_async_copy(held.at[f], out_hbm, sems.at[f]))
        copies[f].start()
    for copy in copies:
        copy.wait()


def total(*parts):
    block = jax.ShapeDtypeStruct((BLOCK, BLOCK, NZ), F32)
    return pl.pallas_call(
        total_kernel,
        out_shape=(block, block),
        in_specs=vmem(5),
        out_specs=(pl.BlockSpec(memory_space=pltpu.HBM),) * 2,
        scratch_shapes=[pltpu.VMEM((2, BLOCK, BLOCK, NZ), F32), pltpu.SemaphoreType.DMA((2,))],
        compiler_params=small,
        name="total",
    )(*parts)


def body(velocity, density, start_pressure, observed, corners):
    own = jnp.stack([velocity, density]).reshape(2 * BLOCK, BLOCK, NZ)
    c = swap(own, "line", False)
    x = swap(own, "line", True)
    yo = swap(own, "shot", True)
    ye = swap(own, "shot", False)
    begun = early(corners, start_pressure, observed)
    passed = onward(x, c)
    yo2 = swap(passed, "shot", True)
    ye2 = swap(passed, "shot", False)
    cyo = swap(yo, "line", False)
    cye = swap(ye, "line", False)
    ce, co, cm, xe, xo, xm, oe, oo, om = wave(begun, own, yo, ye, c, x, ye2, yo2, cye, cyo)
    xo = swap(xo, "shot", True)
    xe = swap(xe, "shot", False)
    ce, co, cm = (swap(block, "line", False) for block in (ce, co, cm))
    oo = swap(merge(co, oo), "shot", True)
    xm, oe = combine(xm, xe, xo, ce, oe)
    xm = swap(xm, "line", True)
    oe = swap(oe, "shot", False)
    return total(om, cm, xm, oe, oo)


def solution(mesh):
    placed = (P("line", "shot", None),) * 5
    return jax.shard_map(
        body,
        mesh=mesh,
        in_specs=placed,
        out_specs=(P("line", "shot", None),) * 2,
        check_vma=False,
    )
```
